32 devices in a mesh: grp: 4 (over y, x), tile: 8 (over z, core).
Axes of the slice: x: 2, y: 2, z: 4, core: 2. Of those that a mesh axis runs over, the one named last changes fastest.
Arguments:
- features: bfloat16 [8192, 128], P(('grp', 'tile')), may hold values from -6 to 6
- source_rows: int32 [27, 64, 128], P(None, ('grp', 'tile')), may hold values from -1 to 127, as said below
- target_codes: int32 [27, 64], P(None, ('grp', 'tile')), may hold values from 0 to 5, as said below
- block_count: int32 [32], P(('grp', 'tile')), may hold values from 1 to 2, as said below
- weight_one: bfloat16 [27, 128, 128], replicated, may hold values from -0.125 to 0.125
- weight_two: bfloat16 [27, 128, 128], replicated, may hold values from -0.125 to 0.125
- out_cotangent: bfloat16 [8192, 128], P(('grp', 'tile')), may hold values from -6 to 6
Outputs:
- block_out: bfloat16 [8192, 128], P(('grp', 'tile'))
- input_grad: bfloat16 [8192, 128], P(('grp', 'tile'))
- wgrad_one: float32 [3456, 128], P('grp')
- wgrad_two: float32 [3456, 128], P('grp')
The draws below stay inside these ranges and needn't reach their ends.
Inputs may be any that keep to these rules, and one draw needn't show every extreme that they name: `source_rows`: entry [k, j, r] is the row of source block j that reaches row r of its target block under offset k, or -1 for none. `target_codes`: a code s * 2 + b names block b of tile t - 1 + s of the same group, t being the source block's tile; offset k = 9 (dx + 1) + 3 (dy + 1) + (dz + 1); s = 1 except s = 0 for offsets with dz = -1 from block 0 of a tile, and s = 2 for offsets with dz = +1 from the last active block of a tile. Blocks of a tile from block_count on are empty.
All inputs are finite; a program needn't handle non-finite values.
Results may differ from the reference program's by a relative error of at most 0.025.
Values may be sent and summed in bfloat16 or wider, within the bound.
No kernel may reach another device: no remote copies, remote signals or barrier semaphores. Data moves between devices by JAX's collectives and lax.ppermute only.
A program may use at most 64 MiB of HBM per device.

```python
import jax
import jax.numpy as jnp
from jax import lax

C = 128
KVOL = 27
BLK = 128
NB = 2
TILES = 32
BLOCKS = 64
VOXELS = 8192
N_GRP = 4
N_TILE = 8


def shared_counts(key):
    return jax.random.randint(jax.random.fold_in(key, 7), (TILES,), 1, NB + 1).astype(jnp.int32)


def draw_block_count(key, part):
    return shared_counts(key)


def draw_target_codes(key, part):
    counts = shared_counts(key)
    target_block = jax.random.randint(jax.random.fold_in(key, 11), (KVOL, BLOCKS), 0, NB).astype(jnp.int32)
    offset_index = jnp.arange(KVOL, dtype=jnp.int32)[:, None]
    block_index = jnp.arange(BLOCKS, dtype=jnp.int32)[None, :]
    within = block_index % NB
    last_active = counts[block_index // NB] - 1
    lower = (offset_index % 3 == 0) & (within == 0)
    upper = (offset_index % 3 == 2) & (within == last_active)
    side = 1 - lower.astype(jnp.int32) + upper.astype(jnp.int32)
    return (side * NB + target_block).astype(jnp.int32)


def draw_source_rows(key, part):
    first, second = jax.random.split(key)
    picked = jax.random.randint(first, (KVOL, BLOCKS, BLK), 0, BLK)
    keeper = jax.random.randint(second, (KVOL, BLOCKS, BLK), 0, 2)
    return jnp.where(keeper == 1, picked, -1).astype(jnp.int32)


def block_scale(rng, extent, cuts, smallest, high):
    gain, own = 1.0, jax.random.fold_in(rng, 6)
    for position, blocks in cuts:
        steps = jnp.exp(jax.random.uniform(jax.random.fold_in(own, position), (blocks,), jnp.float32, smallest / len(cuts), high / len(cuts)))
        gain = gain * jnp.repeat(steps, extent[position] // blocks).reshape([-1 if axis == position else 1 for axis in range(len(extent))])
    return gain


def centred(stream_key, shape, spread, reach, shards=(), kind=jnp.bfloat16):
    loudness = block_scale(stream_key, shape, shards, -0.22, 0.18) if shards else 1.0
    values = jax.random.normal(stream_key, shape, jnp.float32) * spread * loudness
    return jnp.minimum(jnp.maximum(values, -reach), reach).astype(kind)


def setup_inputs(seed: int = 0) -> dict:
    seeds = jax.random.split(jax.random.key(seed), 8)
    features = centred(seeds[0], (VOXELS, C), 1.0, 6.0, ((0, 32),))
    source_rows = draw_source_rows(jax.random.fold_in(seeds[7], 71), 0)
    target_codes = draw_target_codes(jax.random.fold_in(seeds[7], 71), 0)
    block_count = draw_block_count(jax.random.fold_in(seeds[7], 71), 0)
    weight_one = centred(seeds[4], (KVOL, C, C), (14 * C) ** -0.5, 0.125)
    weight_two = centred(seeds[5], (KVOL, C, C), (14 * C) ** -0.5, 0.125)
    out_cotangent = centred(seeds[6], (VOXELS, C), 1.0, 6.0, ((0, 32),))
    return dict(features=features, source_rows=source_rows, target_codes=target_codes, block_count=block_count, weight_one=weight_one, weight_two=weight_two, out_cotangent=out_cotangent)


def silu_grad(values):
    sigma = jax.nn.sigmoid(values)
    return sigma * (1.0 + values * (1.0 - sigma))

def tile_gather(field, row_map, active):
    offsets, blocks_dev, block_rows = row_map.shape
    valid_rows = (row_map >= 0) & active[None, :, None]
    flat_rows = (jnp.arange(blocks_dev, dtype=jnp.int32)[None, :, None] * block_rows + jnp.maximum(row_map, 0)).astype(jnp.int32).reshape(-1)
    picked = jnp.take(field, flat_rows, axis=0).reshape(offsets, blocks_dev * block_rows, -1)
    valid_mask = valid_rows.reshape(offsets, blocks_dev * block_rows, 1)
    picked = jnp.where(valid_mask, picked, jnp.zeros_like(picked))
    return (picked, flat_rows, valid_mask)

def tile_spread(picked, weights, codes):
    offsets, total_rows, channels = picked.shape
    blocks_dev = codes.shape[1]
    block_rows = total_rows // blocks_dev
    partial_value = jnp.einsum('kmc,kcd->kmd', picked.astype(jnp.float32), weights.astype(jnp.float32), precision=lax.Precision.HIGHEST)
    one_hot = (codes[:, :, None] == jnp.arange(3 * blocks_dev, dtype=jnp.int32)[None, None, :]).astype(jnp.float32)
    buffer = jnp.einsum('kis,kirc->src', one_hot, partial_value.reshape(offsets, blocks_dev, block_rows, -1), precision=lax.Precision.HIGHEST)
    return buffer.reshape(3, blocks_dev * block_rows, -1)

def tile_pull(stacked, codes, picked, flat_rows, valid_mask, weights):
    offsets, total_rows, channels = picked.shape
    blocks_dev = codes.shape[1]
    grid_blocks = stacked.reshape(3 * blocks_dev, total_rows // blocks_dev, -1)
    grad_rows = jnp.take(grid_blocks, codes.reshape(-1).astype(jnp.int32), axis=0).reshape(offsets, total_rows, -1)
    wgrad = jnp.einsum('kmc,kmd->kcd', picked.astype(jnp.float32), grad_rows.astype(jnp.float32), precision=lax.Precision.HIGHEST)
    grad_pick = jnp.einsum('kmd,kcd->kmc', grad_rows.astype(jnp.float32), weights.astype(jnp.float32), precision=lax.Precision.HIGHEST)
    grad_pick = jnp.where(valid_mask, grad_pick, jnp.zeros_like(grad_pick))
    grad_in = jnp.zeros((total_rows, channels), jnp.float32).at[flat_rows].add(grad_pick.reshape(-1, channels))
    return (wgrad, grad_in)

def join_partials(buffer):
    zero_tile = jnp.zeros_like(buffer[:1, 0])
    from_next = jnp.concatenate([buffer[1:, 0], zero_tile], axis=0)
    from_prev = jnp.concatenate([zero_tile, buffer[:-1, 2]], axis=0)
    return buffer[:, 1] + from_next + from_prev

def neighbor_rows(grads):
    zero_tile = jnp.zeros_like(grads[:1])
    before = jnp.concatenate([zero_tile, grads[:-1]], axis=0)
    after = jnp.concatenate([grads[1:], zero_tile], axis=0)
    return jnp.concatenate([before, grads, after], axis=1)

def group_pass(feature_grid, row_maps, code_grid, count_grid, cotangent, weight_one, weight_two):
    blocks_dev = code_grid.shape[2]
    block_rows = row_maps.shape[3]
    active = jnp.arange(blocks_dev, dtype=jnp.int32)[None, :] < count_grid[:, None]
    row_mask = jnp.repeat(active, block_rows, axis=1).astype(jnp.float32)[:, :, None]
    pick_in, flat_rows, valid_mask = jax.vmap(tile_gather)(feature_grid, row_maps, active)
    pre_one = join_partials(jax.vmap(lambda p, c: tile_spread(p, weight_one, c))(pick_in, code_grid))
    hidden = (jax.nn.silu(pre_one) * row_mask).astype(jnp.bfloat16)
    pick_mid = jax.vmap(lambda h, r, a: tile_gather(h, r, a)[0])(hidden, row_maps, active)
    total = join_partials(jax.vmap(lambda p, c: tile_spread(p, weight_two, c))(pick_mid, code_grid)) + feature_grid.astype(jnp.float32)
    result = (jax.nn.silu(total) * row_mask).astype(jnp.bfloat16)
    grad_sum = (cotangent.astype(jnp.float32) * silu_grad(total) * row_mask).astype(jnp.bfloat16)
    wgrad_two, grad_mid = jax.vmap(lambda s, c, p, f, v: tile_pull(s, c, p, f, v, weight_two))(neighbor_rows(grad_sum), code_grid, pick_mid, flat_rows, valid_mask)
    grad_pre = (grad_mid * silu_grad(pre_one) * row_mask).astype(jnp.bfloat16)
    wgrad_one, grad_conv = jax.vmap(lambda s, c, p, f, v: tile_pull(s, c, p, f, v, weight_one))(neighbor_rows(grad_pre), code_grid, pick_in, flat_rows, valid_mask)
    input_grad = (grad_conv + grad_sum.astype(jnp.float32)).astype(jnp.bfloat16)
    return (result, input_grad, lax.optimization_barrier(jnp.sum(wgrad_one, axis=0)), lax.optimization_barrier(jnp.sum(wgrad_two, axis=0)))

def reference(features, source_rows, target_codes, block_count, weight_one, weight_two, out_cotangent):
    groups = N_GRP
    tiles = N_TILE
    feature_grid = features.reshape(groups, tiles, NB * BLK, C)
    row_maps = source_rows.reshape(KVOL, groups, tiles, NB, BLK).transpose(1, 2, 0, 3, 4)
    code_grid = target_codes.reshape(KVOL, groups, tiles, NB).transpose(1, 2, 0, 3)
    count_grid = block_count.reshape(groups, tiles)
    cotangent = out_cotangent.reshape(groups, tiles, NB * BLK, C)
    result, input_grad, sums_one, sums_two = lax.map(lambda a: group_pass(a[0], a[1], a[2], a[3], a[4], weight_one, weight_two), (feature_grid, row_maps, code_grid, count_grid, cotangent))
    scale = float(VOXELS) ** (-0.5)
    wgrad_one = (lax.optimization_barrier(jnp.sum(sums_one, axis=0)) * scale).reshape(KVOL * C, C)
    wgrad_two = (lax.optimization_barrier(jnp.sum(sums_two, axis=0)) * scale).reshape(KVOL * C, C)
    return (result.reshape(VOXELS, C), input_grad.reshape(VOXELS, C), wgrad_one, wgrad_two)
```

```python
import jax
import jax.numpy as jnp
from jax import lax
from jax.experimental import pallas as pl
from jax.experimental.pallas import tpu as pltpu
from jax.sharding import PartitionSpec as P

F32 = jnp.float32
BF16 = jnp.bfloat16
KINDS = 3
LIMIT = 28 * 1024 * 1024
NT = (((1,), (1,)), ((), ()))


def swapped(value, axis, bits):
    count = lax.axis_size(axis)
    return lax.ppermute(value, axis, [(i, i ^ bits) for i in range(count) if i ^ bits < count])


def crossed(value):
    count = lax.axis_size("tile")
    pairs = [(i, ((i + 1) ^ 1) - 1) for i in range(count)]
    return lax.ppermute(value, "tile", [(i, j) for i, j in pairs if 0 <= j < count])


def sigmoid_terms(values):
    sigma = jax.nn.sigmoid(values)
    return values * sigma, sigma * (1.0 + values * (1.0 - sigma))


def halo_sides(odd, core, cross):
    return jnp.where(odd, cross, core), jnp.where(odd, core, cross)


def row_mask(rows, blk, count):
    block = lax.broadcasted_iota(jnp.int32, (rows, 1), 0) // blk
    return (block < count).astype(F32)


def pack_kernel(info, features, source_rows, codes, entries, core_out, cross_out):
    offsets, _, blk = source_rows.shape
    per = offsets // KINDS
    odd, count = info[0] == 1, info[1]
    coded = []
    for j in range(2):
        rows = source_rows[:, j, :]
        block = lax.rem(codes[:, j : j + 1], 2)
        live = (rows >= 0) & (count > j)
        coded.append(jnp.where(live, rows + blk * block, -1).astype(F32))
    first, second = coded
    both = count == 2
    entries[0] = first
    entries[1] = second
    to_prev = jnp.concatenate([first[i * KINDS : i * KINDS + 1] for i in range(per)], axis=0)
    last = jnp.where(both, second, first)
    to_next = jnp.concatenate([last[i * KINDS + 2 : i * KINDS + 3] for i in range(per)], axis=0)
    front, back = features[:blk, :], features[blk:, :]
    tail = jnp.where(both, back, front)
    pad = core_out.shape[0] - blk - per
    fill = jnp.full((pad, blk), -1.0, F32)
    to_prev = jnp.concatenate([to_prev, fill], axis=0).astype(BF16)
    to_next = jnp.concatenate([to_next, fill], axis=0).astype(BF16)
    core_out[:blk, :] = jnp.where(odd, front, tail)
    cross_out[:blk, :] = jnp.where(odd, tail, front)
    core_out[blk:, :] = jnp.where(odd, to_prev, to_next)
    cross_out[blk:, :] = jnp.where(odd, to_next, to_prev)


def targets_by_sources(columns, kind, per, index, blk):
    lane = lax.broadcasted_iota(jnp.int32, (blk, blk), 1).astype(F32)
    halves = []
    for side in range(2):
        at = (kind * 2 + side) * per + index
        entry = jnp.broadcast_to(columns[:, at : at + 1], (blk, blk))
        halves.append(jnp.concatenate([entry, entry - blk], axis=0))
    wide = jnp.concatenate([lane, lane], axis=0)
    parts = [jnp.where(half == wide, 1.0, 0.0).astype(BF16) for half in halves]
    return jnp.concatenate(parts, axis=1)


def sources_by_targets(entries, kind, per, index, blk):
    sub = lax.broadcasted_iota(jnp.int32, (blk, 2 * blk), 0).astype(F32)
    parts = []
    for side in range(2):
        at = (kind * 2 + side) * per + index
        row = entries[at : at + 1, :]
        wide = jnp.concatenate([row, row - blk], axis=1)
        parts.append(jnp.where(wide == sub, 1.0, 0.0).astype(BF16))
    return jnp.concatenate(parts, axis=0)


def convolve(columns, sources, weights, picked):
    blk, channels = columns.shape[0], weights.shape[1]
    per = picked.shape[1] // channels // KINDS
    for kind in range(KINDS):
        for i in range(per):
            select = targets_by_sources(columns, kind, per, i, blk)
            got = jnp.dot(select, sources[kind], preferred_element_type=F32)
            at = (i * KINDS + kind) * channels
            picked[:, at : at + channels] = got.astype(BF16)
    return jnp.dot(picked[...], weights[...], preferred_element_type=F32)


def pull_back(entries, grads, weights, sources, pulled, wgrad):
    blk, channels = entries.shape[1], grads.shape[1]
    per = pulled.shape[1] // channels // KINDS
    sums = []
    for kind in range(KINDS):
        base = kind * per * channels
        for i in range(per):
            select = sources_by_targets(entries, kind, per, i, blk)
            got = jnp.dot(select, grads, preferred_element_type=F32)
            at = base + i * channels
            pulled[:, at : at + channels] = got.astype(BF16)
        held = pulled[:, base : base + per * channels]
        wide = jnp.concatenate(
            [
                weights[(i * KINDS + kind) * channels : (i * KINDS + kind + 1) * channels, :]
                for i in range(per)
            ],
            axis=1,
        )
        sums.append(lax.dot_general(held, wide, NT, preferred_element_type=F32))
        turned = sources[kind].T
        terms = jnp.dot(turned, held, preferred_element_type=F32)
        for i in range(per):
            at = (i * KINDS + kind) * channels
            wgrad[at : at + channels, :] = terms[:, i * channels : (i + 1) * channels]
    return sums


def split_sums(sums, both, blk):
    low, mid, high = sums
    first = mid[:blk] + jnp.where(both, high[blk:], 0.0)
    second = mid[blk:] + low[blk:]
    return jnp.concatenate([first, second], axis=0), low[:blk], high[:blk]


def halves_out(odd_bit, wgrad, keep, send, at):
    shards, slot, _ = keep.shape
    rows = wgrad.shape[0] // shards // 2
    for s in range(shards):
        mine = pl.ds(s * 2 * rows + odd_bit * rows, rows)
        other = pl.ds(s * 2 * rows + (1 - odd_bit) * rows, rows)
        keep[s, :rows, :] = wgrad[mine, :]
        start = at + s * slot
        send[start : start + rows, :] = wgrad[other, :].astype(BF16)


def first_kernel(
    info, local, features, core_in, cross_in, weights,
    entries, halo, hidden, slope, core_out, cross_out, picked,
):
    blk = features.shape[0] // 2
    per = local.shape[1] // KINDS
    odd, count = info[0] == 1, info[1]
    both = count == 2
    from_next, from_prev = halo_sides(odd, core_in[...].astype(F32), cross_in[...].astype(F32))
    first, second = local[0], local[1]

    def of_kind(values, kind):
        return [values[i * KINDS + kind : i * KINDS + kind + 1] for i in range(per)]

    rows = [from_next[blk : blk + per]]
    rows += of_kind(second, 0) + of_kind(first, 1) + of_kind(second, 1)
    rows += [from_prev[blk : blk + per]]
    rows += of_kind(jnp.where(both, first, -1.0), 2)
    table = jnp.concatenate(rows, axis=0)
    entries[...] = table
    spare = -table.shape[0] % 8
    table = jnp.concatenate([table, jnp.zeros((spare, blk), F32)], axis=0)
    columns = table.T
    after, before = from_next[:blk].astype(BF16), from_prev[:blk].astype(BF16)
    halo[0] = after
    halo[1] = before
    front, back = features[:blk, :], features[blk:, :]
    sources = [
        jnp.concatenate([after, back], axis=0),
        features[...],
        jnp.concatenate([before, front], axis=0),
    ]
    pre = convolve(columns, sources, weights, picked)
    mask = row_mask(2 * blk, blk, count)
    value, grad = sigmoid_terms(pre)
    field = (value * mask).astype(BF16)
    hidden[...] = field
    slope[...] = grad * mask
    head = field[:blk]
    tail = jnp.where(both, field[blk:], head)
    core_out[...] = jnp.where(odd, head, tail)
    cross_out[...] = jnp.where(odd, tail, head)


def exchange_sides(odd, to_next, to_prev):
    return jnp.where(odd, to_prev, to_next), jnp.where(odd, to_next, to_prev)


def second_kernel(
    info, entries, features, hidden, core_in, cross_in, weights, cotangent,
    result, grads_out, own_out, keep, core_out, cross_out, picked, pulled, wgrad,
):
    blk = features.shape[0] // 2
    odd, count = info[0] == 1, info[1]
    both = count == 2
    after, before = halo_sides(odd, core_in[...], cross_in[...])
    front, back = hidden[:blk, :], hidden[blk:, :]
    sources = [
        jnp.concatenate([after, back], axis=0),
        hidden[...],
        jnp.concatenate([before, front], axis=0),
    ]
    table = entries[...]
    spare = -table.shape[0] % 8
    columns = jnp.concatenate([table, jnp.zeros((spare, blk), F32)], axis=0).T
    total = convolve(columns, sources, weights, picked) + features[...].astype(F32)
    mask = row_mask(2 * blk, blk, count)
    value, grad = sigmoid_terms(total)
    result[...] = (value * mask).astype(BF16)
    grads = (cotangent[...].astype(F32) * grad * mask).astype(BF16)
    grads_out[...] = grads
    sums = pull_back(entries, grads, weights, sources, pulled, wgrad)
    own, to_next, to_prev = split_sums(sums, both, blk)
    own_out[...] = own
    core, cross = exchange_sides(odd, to_next, to_prev)
    core_out[:blk, :] = core.astype(BF16)
    cross_out[...] = cross.astype(BF16)
    halves_out(info[0], wgrad, keep, core_out, blk)


def joined(own, odd, both, core_in, cross_in, blk):
    from_next, from_prev = halo_sides(odd, core_in, cross_in)
    first = own[:blk] + from_prev + jnp.where(both, 0.0, from_next)
    second = own[blk:] + jnp.where(both, from_next, 0.0)
    return jnp.concatenate([first, second], axis=0)


def third_kernel(
    info, entries, features, halo, own, core_in, cross_in, slope, grads_in, weights,
    own_out, keep, core_out, cross_out, pulled, wgrad,
):
    blk = features.shape[0] // 2
    odd, both = info[0] == 1, info[1] == 2
    core, cross = core_in[:blk, :].astype(F32), cross_in[...].astype(F32)
    summed = joined(own[...], odd, both, core, cross, blk)
    grads = (summed * slope[...]).astype(BF16)
    sources = [
        jnp.concatenate([halo[0], features[blk:, :]], axis=0),
        features[...],
        jnp.concatenate([halo[1], features[:blk, :]], axis=0),
    ]
    sums = pull_back(entries, grads, weights, sources, pulled, wgrad)
    own_sum, to_next, to_prev = split_sums(sums, both, blk)
    own_out[...] = own_sum + grads_in[...].astype(F32)
    core, cross = exchange_sides(odd, to_next, to_prev)
    core_out[:blk, :] = core.astype(BF16)
    cross_out[...] = cross.astype(BF16)
    halves_out(info[0], wgrad, keep, core_out, blk)


def last_kernel(info, own, core_in, cross_in, input_grad):
    blk = own.shape[0] // 2
    odd, both = info[0] == 1, info[1] == 2
    core, cross = core_in[:blk, :].astype(F32), cross_in[...].astype(F32)
    input_grad[...] = joined(own[...], odd, both, core, cross, blk).astype(BF16)


def shards_kernel(info, keep_one, keep_two, core_one, core_two, own, *sends):
    shards, slot, _ = keep_one.shape
    blk = core_one.shape[0] - shards * slot
    me = info[2]
    for d in range(shards):
        to = me ^ d
        at = pl.ds(pl.multiple_of(blk + to * slot, 16), slot)
        for half, keep, core in ((0, keep_one, core_one), (1, keep_two, core_two)):
            value = keep[to] + core[at, :].astype(F32)
            if d == 0:
                own[half] = value
            else:
                sends[d - 1][half] = value.astype(BF16)


def call(kernel, outs, *args, scratch=()):
    specs = [pl.BlockSpec(memory_space=pltpu.SMEM)]
    specs += [pl.BlockSpec(memory_space=pltpu.VMEM)] * (len(args) - 1)
    return pl.pallas_call(
        kernel,
        out_shape=[jax.ShapeDtypeStruct(shape, kind) for shape, kind in outs],
        in_specs=specs,
        out_specs=[pl.BlockSpec(memory_space=pltpu.VMEM)] * len(outs),
        scratch_shapes=[pltpu.VMEM(shape, kind) for shape, kind in scratch],
        compiler_params=pltpu.CompilerParams(vmem_limit_bytes=LIMIT),
    )(*args)


def on_device(
    features, source_rows, target_codes, block_count, weight_one, weight_two, out_cotangent
):
    offsets, blocks_dev, blk = source_rows.shape
    rows, channels = features.shape
    n_grp, n_tile = lax.axis_size("grp"), lax.axis_size("tile")
    per = offsets // KINDS
    info = jnp.stack(
        [lax.axis_index("tile") % 2, block_count[0], lax.axis_index("grp")]
    ).astype(jnp.int32)
    flat_one = weight_one.reshape(offsets * channels, channels)
    flat_two = weight_two.reshape(offsets * channels, channels)
    packed = blk + per + (-per % 16)
    half = offsets * channels // n_grp // 2
    wide = (rows, offsets * channels)
    field, block = ((rows, channels), BF16), ((blk, channels), BF16)
    summed = ((rows, channels), F32)
    slot = half + (-half % 16)
    keep_shape = ((n_grp, slot, channels), F32)
    core_shape = ((blk + n_grp * slot, channels), BF16)

    local, core, cross = call(
        pack_kernel,
        [((2, offsets, blk), F32), ((packed, channels), BF16), ((packed, channels), BF16)],
        info, features, source_rows, target_codes,
    )
    cross, core = crossed(cross), swapped(core, "tile", 1)
    entries, halo, hidden, slope, core, cross = call(
        first_kernel,
        [((2 * offsets, blk), F32), ((2, blk, channels), BF16), field, summed, block, block],
        info, local, features, core, cross, flat_one,
        scratch=[(wide, BF16)],
    )
    cross, core = crossed(cross), swapped(core, "tile", 1)
    result, grad_sum, own, keep_two, core_two, cross = call(
        second_kernel,
        [field, field, summed, keep_shape, core_shape, block],
        info, entries, features, hidden, core, cross, flat_two, out_cotangent,
        scratch=[(wide, BF16), (wide, BF16), ((offsets * channels, channels), F32)],
    )
    cross, core_two = crossed(cross), swapped(core_two, "tile", 1)
    own, keep_one, core_one, cross = call(
        third_kernel,
        [summed, keep_shape, core_shape, block],
        info, entries, features, halo, own, core_two, cross, slope, grad_sum, flat_one,
        scratch=[(wide, BF16), ((offsets * channels, channels), F32)],
    )
    core_one = swapped(core_one, "tile", 1)
    shard = (2, slot, channels)
    mine, *sends = call(
        shards_kernel,
        [(shard, F32)] + [(shard, BF16)] * (n_grp - 1),
        info, keep_one, keep_two, core_one, core_two,
    )
    for d, send in enumerate(sends):
        mine = mine + swapped(send, "grp", d + 1).astype(F32)
    cross = crossed(cross)
    (input_grad,) = call(last_kernel, [field], info, own, core_one, cross)
    bits = 2
    while bits < n_tile:
        mine = mine.astype(BF16)
        mine = mine.astype(F32) + swapped(mine, "tile", bits).astype(F32)
        bits *= 2
    voxel_total = n_grp * n_tile * rows
    mine = mine[:, :half] * float(voxel_total) ** (-0.5)
    other = swapped(mine, "tile", 1)
    odd = lax.axis_index("tile") % 2 == 1
    whole = jnp.concatenate(
        [jnp.where(odd, other, mine), jnp.where(odd, mine, other)], axis=1
    )
    return (result, input_grad, whole[0], whole[1])


def solution(mesh):
    in_specs = (
        P(("grp", "tile"), None),
        P(None, ("grp", "tile"), None),
        P(None, ("grp", "tile")),
        P(("grp", "tile")),
        P(),
        P(),
        P(("grp", "tile"), None),
    )
    out_specs = (P(("grp", "tile"), None), P(("grp", "tile"), None), P("grp", None), P("grp", None))
    return jax.shard_map(
        on_device, mesh=mesh, in_specs=in_specs, out_specs=out_specs, check_vma=False
    )
```

```python
import jax
import jax.numpy as jnp
from jax import lax
from jax.experimental import pallas as pl
from jax.experimental.pallas import tpu as pltpu
from jax.sharding import PartitionSpec as P

F32 = jnp.float32
BF16 = jnp.bfloat16
KINDS = 3
LIMIT = 28 * 1024 * 1024
NT = (((1,), (1,)), ((), ()))


def swapped(value, axis, bits):
    count = lax.axis_size(axis)
    return lax.ppermute(value, axis, [(i, i ^ bits) for i in range(count) if i ^ bits < count])


def crossed(value):
    groups, count = lax.axis_size("grp"), lax.axis_size("tile")
    pairs = []
    for i in range(groups * count):
        group, tile = divmod(i, count)
        other = ((tile + 1) ^ 1) - 1
        if 0 <= other < count:
            pairs.append((i, group * count + other))
        elif (group ^ 1) < groups:
            pairs.append((i, (group ^ 1) * count + tile))
    return lax.ppermute(value, ("grp", "tile"), pairs)


def sigmoid_terms(values):
    sigma = jax.nn.sigmoid(values)
    return values * sigma, sigma * (1.0 + values * (1.0 - sigma))


def halo_sides(odd, core, cross):
    return jnp.where(odd, cross, core), jnp.where(odd, core, cross)


def row_mask(rows, blk, count):
    block = lax.broadcasted_iota(jnp.int32, (rows, 1), 0) // blk
    return (block < count).astype(F32)


def pack_kernel(info, features, source_rows, codes, entries, core_out, cross_out):
    offsets, _, blk = source_rows.shape
    per = offsets // KINDS
    odd, count = info[0] == 1, info[1]
    coded = []
    for j in range(2):
        rows = source_rows[:, j, :]
        block = lax.rem(codes[:, j : j + 1], 2)
        live = (rows >= 0) & (count > j)
        coded.append(jnp.where(live, rows + blk * block, -1).astype(F32))
    first, second = coded
    both = count == 2
    entries[0] = first
    entries[1] = second
    head = jnp.where(info[3] == 0, -1.0, first)
    to_prev = jnp.concatenate([head[i * KINDS : i * KINDS + 1] for i in range(per)], axis=0)
    last = jnp.where(info[3] == 1, -1.0, jnp.where(both, second, first))
    to_next = jnp.concatenate([last[i * KINDS + 2 : i * KINDS + 3] for i in range(per)], axis=0)
    front, back = features[:blk, :], features[blk:, :]
    tail = jnp.where(both, back, front)
    pad = core_out.shape[0] - blk - per
    fill = jnp.full((pad, blk), -1.0, F32)
    to_prev = jnp.concatenate([to_prev, fill], axis=0).astype(BF16)
    to_next = jnp.concatenate([to_next, fill], axis=0).astype(BF16)
    core_out[:blk, :] = jnp.where(odd, front, tail)
    cross_out[:blk, :] = jnp.where(odd, tail, front)
    core_out[blk:, :] = jnp.where(odd, to_prev, to_next)
    cross_out[blk:, :] = jnp.where(odd, to_next, to_prev)


def targets_by_sources(columns, kind, per, index, blk):
    lane = lax.broadcasted_iota(jnp.int32, (blk, blk), 1).astype(F32)
    halves = []
    for side in range(2):
        at = (kind * 2 + side) * per + index
        entry = jnp.broadcast_to(columns[:, at : at + 1], (blk, blk))
        halves.append(jnp.concatenate([entry, entry - blk], axis=0))
    wide = jnp.concatenate([lane, lane], axis=0)
    parts = [jnp.where(half == wide, 1.0, 0.0).astype(BF16) for half in halves]
    return jnp.concatenate(parts, axis=1)


def sources_by_targets(entries, kind, per, index, blk):
    sub = lax.broadcasted_iota(jnp.int32, (blk, 2 * blk), 0).astype(F32)
    parts = []
    for side in range(2):
        at = (kind * 2 + side) * per + index
        row = entries[at : at + 1, :]
        wide = jnp.concatenate([row, row - blk], axis=1)
        parts.append(jnp.where(wide == sub, 1.0, 0.0).astype(BF16))
    return jnp.concatenate(parts, axis=0)


def convolve(columns, sources, weights, picked):
    blk, channels = columns.shape[0], weights.shape[1]
    per = picked.shape[1] // channels // KINDS
    for kind in range(KINDS):
        for i in range(per):
            select = targets_by_sources(columns, kind, per, i, blk)
            got = jnp.dot(select, sources[kind], preferred_element_type=F32)
            at = (i * KINDS + kind) * channels
            picked[:, at : at + channels] = got.astype(BF16)
    return jnp.dot(picked[...], weights[...], preferred_element_type=F32)


def pull_back(entries, grads, weights, sources, pulled, wgrad):
    blk, channels = entries.shape[1], grads.shape[1]
    per = pulled.shape[1] // channels // KINDS
    sums = []
    for kind in range(KINDS):
        base = kind * per * channels
        for i in range(per):
            select = sources_by_targets(entries, kind, per, i, blk)
            got = jnp.dot(select, grads, preferred_element_type=F32)
            at = base + i * channels
            pulled[:, at : at + channels] = got.astype(BF16)
        held = pulled[:, base : base + per * channels]
        wide = jnp.concatenate(
            [
                weights[(i * KINDS + kind) * channels : (i * KINDS + kind + 1) * channels, :]
                for i in range(per)
            ],
            axis=1,
        )
        sums.append(lax.dot_general(held, wide, NT, preferred_element_type=F32))
        turned = sources[kind].T
        terms = jnp.dot(turned, held, preferred_element_type=F32)
        for i in range(per):
            at = (i * KINDS + kind) * channels
            wgrad[at : at + channels, :] = terms[:, i * channels : (i + 1) * channels]
    return sums


def split_sums(sums, both, blk):
    low, mid, high = sums
    first = mid[:blk] + jnp.where(both, high[blk:], 0.0)
    second = mid[blk:] + low[blk:]
    return jnp.concatenate([first, second], axis=0), low[:blk], high[:blk]


def halves_out(odd_bit, wgrad, keep, send, at):
    shards, slot, _ = keep.shape
    rows = wgrad.shape[0] // shards // 2
    for s in range(shards):
        mine = pl.ds(s * 2 * rows + odd_bit * rows, rows)
        other = pl.ds(s * 2 * rows + (1 - odd_bit) * rows, rows)
        keep[s, :rows, :] = wgrad[mine, :]
        start = at + s * slot
        send[start : start + rows, :] = wgrad[other, :].astype(BF16)


def first_kernel(
    info, local, features, core_in, cross_in, weights,
    entries, halo, hidden, slope, core_out, cross_out, picked,
):
    blk = features.shape[0] // 2
    per = local.shape[1] // KINDS
    odd, count = info[0] == 1, info[1]
    both = count == 2
    from_next, from_prev = halo_sides(odd, core_in[...].astype(F32), cross_in[...].astype(F32))
    first, second = local[0], local[1]

    def of_kind(values, kind):
        return [values[i * KINDS + kind : i * KINDS + kind + 1] for i in range(per)]

    rows = [from_next[blk : blk + per]]
    rows += of_kind(second, 0) + of_kind(first, 1) + of_kind(second, 1)
    rows += [from_prev[blk : blk + per]]
    rows += of_kind(jnp.where(both, first, -1.0), 2)
    table = jnp.concatenate(rows, axis=0)
    entries[...] = table
    spare = -table.shape[0] % 8
    table = jnp.concatenate([table, jnp.zeros((spare, blk), F32)], axis=0)
    columns = table.T
    after, before = from_next[:blk].astype(BF16), from_prev[:blk].astype(BF16)
    halo[0] = after
    halo[1] = before
    front, back = features[:blk, :], features[blk:, :]
    sources = [
        jnp.concatenate([after, back], axis=0),
        features[...],
        jnp.concatenate([before, front], axis=0),
    ]
    pre = convolve(columns, sources, weights, picked)
    mask = row_mask(2 * blk, blk, count)
    value, grad = sigmoid_terms(pre)
    field = (value * mask).astype(BF16)
    hidden[...] = field
    slope[...] = grad * mask
    head = field[:blk]
    tail = jnp.where(both, field[blk:], head)
    core_out[...] = jnp.where(odd, head, tail)
    cross_out[...] = jnp.where(odd, tail, head)


def exchange_sides(odd, to_next, to_prev):
    return jnp.where(odd, to_prev, to_next), jnp.where(odd, to_next, to_prev)


def second_kernel(
    info, entries, features, hidden, core_in, cross_in, weights, cotangent,
    result, grads_out, own_out, keep, core_out, cross_out, picked, pulled, wgrad,
):
    blk = features.shape[0] // 2
    odd, count = info[0] == 1, info[1]
    both = count == 2
    after, before = halo_sides(odd, core_in[...], cross_in[...])
    front, back = hidden[:blk, :], hidden[blk:, :]
    sources = [
        jnp.concatenate([after, back], axis=0),
        hidden[...],
        jnp.concatenate([before, front], axis=0),
    ]
    table = entries[...]
    spare = -table.shape[0] % 8
    columns = jnp.concatenate([table, jnp.zeros((spare, blk), F32)], axis=0).T
    total = convolve(columns, sources, weights, picked) + features[...].astype(F32)
    mask = row_mask(2 * blk, blk, count)
    value, grad = sigmoid_terms(total)
    result[...] = (value * mask).astype(BF16)
    grads = (cotangent[...].astype(F32) * grad * mask).astype(BF16)
    grads_out[...] = grads
    sums = pull_back(entries, grads, weights, sources, pulled, wgrad)
    own, to_next, to_prev = split_sums(sums, both, blk)
    own_out[...] = own
    core, cross = exchange_sides(odd, to_next, to_prev)
    core_out[:blk, :] = core.astype(BF16)
    cross_out[...] = cross.astype(BF16)
    halves_out(info[0], wgrad, keep, core_out, blk)


def joined(own, odd, both, core_in, cross_in, blk):
    from_next, from_prev = halo_sides(odd, core_in, cross_in)
    first = own[:blk] + from_prev + jnp.where(both, 0.0, from_next)
    second = own[blk:] + jnp.where(both, from_next, 0.0)
    return jnp.concatenate([first, second], axis=0)


def third_kernel(
    info, entries, features, halo, own, core_in, cross_in, slope, grads_in, weights,
    own_out, keep, core_out, cross_out, pulled, wgrad,
):
    blk = features.shape[0] // 2
    odd, both = info[0] == 1, info[1] == 2
    core, cross = core_in[:blk, :].astype(F32), cross_in[...].astype(F32)
    summed = joined(own[...], odd, both, core, cross, blk)
    grads = (summed * slope[...]).astype(BF16)
    sources = [
        jnp.concatenate([halo[0], features[blk:, :]], axis=0),
        features[...],
        jnp.concatenate([halo[1], features[:blk, :]], axis=0),
    ]
    sums = pull_back(entries, grads, weights, sources, pulled, wgrad)
    own_sum, to_next, to_prev = split_sums(sums, both, blk)
    own_out[...] = own_sum + grads_in[...].astype(F32)
    core, cross = exchange_sides(odd, to_next, to_prev)
    core_out[:blk, :] = core.astype(BF16)
    cross_out[...] = cross.astype(BF16)
    halves_out(info[0], wgrad, keep, core_out, blk)


def last_kernel(info, own, core_in, cross_in, input_grad):
    blk = own.shape[0] // 2
    odd, both = info[0] == 1, info[1] == 2
    core, cross = core_in[:blk, :].astype(F32), cross_in[...].astype(F32)
    input_grad[...] = joined(own[...], odd, both, core, cross, blk).astype(BF16)


def shards_kernel(info, keep_one, keep_two, core_one, core_two, own, *sends):
    shards, slot, _ = keep_one.shape
    blk = core_one.shape[0] - shards * slot
    me = info[2]
    for d in range(shards):
        to = me ^ d
        at = pl.ds(pl.multiple_of(blk + to * slot, 16), slot)
        for half, keep, core in ((0, keep_one, core_one), (1, keep_two, core_two)):
            value = keep[to] + core[at, :].astype(F32)
            if d == 0:
                own[half] = value
            else:
                sends[d - 1][half] = value.astype(BF16)


def call(kernel, outs, *args, scratch=(), micros=1):
    specs = [pl.BlockSpec(memory_space=pltpu.SMEM)]
    specs += [pl.BlockSpec(memory_space=pltpu.VMEM)] * (len(args) - 1)
    return pl.pallas_call(
        kernel,
        out_shape=[jax.ShapeDtypeStruct(shape, kind) for shape, kind in outs],
        in_specs=specs,
        out_specs=[pl.BlockSpec(memory_space=pltpu.VMEM)] * len(outs),
        scratch_shapes=[pltpu.VMEM(shape, kind) for shape, kind in scratch],
        compiler_params=pltpu.CompilerParams(vmem_limit_bytes=LIMIT),
        cost_estimate=pl.CostEstimate(
            flops=micros * 10**9, bytes_accessed=micros * 3 * 10**6, transcendentals=0
        ),
    )(*args)


def on_device(
    features, source_rows, target_codes, block_count, weight_one, weight_two, out_cotangent
):
    offsets, blocks_dev, blk = source_rows.shape
    rows, channels = features.shape
    n_grp, n_tile = lax.axis_size("grp"), lax.axis_size("tile")
    per = offsets // KINDS
    tile = lax.axis_index("tile")
    end = jnp.where(tile == 0, 0, jnp.where(tile == n_tile - 1, 1, 2))
    info = jnp.stack([tile % 2, block_count[0], lax.axis_index("grp"), end]).astype(jnp.int32)
    flat_one = weight_one.reshape(offsets * channels, channels)
    flat_two = weight_two.reshape(offsets * channels, channels)
    packed = blk + per + (-per % 16)
    half = offsets * channels // n_grp // 2
    wide = (rows, offsets * channels)
    field, block = ((rows, channels), BF16), ((blk, channels), BF16)
    summed = ((rows, channels), F32)
    slot = half + (-half % 16)
    keep_shape = ((n_grp, slot, channels), F32)
    core_shape = ((blk + n_grp * slot, channels), BF16)

    local, core, cross = call(
        pack_kernel,
        [((2, offsets, blk), F32), ((packed, channels), BF16), ((packed, channels), BF16)],
        info, features, source_rows, target_codes,
        micros=3,
    )
    cross, core = crossed(cross), swapped(core, "tile", 1)
    entries, halo, hidden, slope, core, cross = call(
        first_kernel,
        [((2 * offsets, blk), F32), ((2, blk, channels), BF16), field, summed, block, block],
        info, local, features, core, cross, flat_one,
        scratch=[(wide, BF16)],
        micros=3,
    )
    cross, core = crossed(cross), swapped(core, "tile", 1)
    result, grad_sum, own, keep_two, core_two, cross = call(
        second_kernel,
        [field, field, summed, keep_shape, core_shape, block],
        info, entries, features, hidden, core, cross, flat_two, out_cotangent,
        scratch=[(wide, BF16), (wide, BF16), ((offsets * channels, channels), F32)],
        micros=5,
    )
    cross, core_two = crossed(cross), swapped(core_two, "tile", 1)
    own, keep_one, core_one, cross = call(
        third_kernel,
        [summed, keep_shape, core_shape, block],
        info, entries, features, halo, own, core_two, cross, slope, grad_sum, flat_one,
        scratch=[(wide, BF16), ((offsets * channels, channels), F32)],
    )
    core_one = swapped(core_one, "tile", 1)
    shard = (2, slot, channels)
    mine, *sends = call(
        shards_kernel,
        [(shard, F32)] + [(shard, BF16)] * (n_grp - 1),
        info, keep_one, keep_two, core_one, core_two,
    )
    cross, *sends = lax.optimization_barrier((cross, *sends))
    got = [swapped(send, "grp", d + 1) for d, send in enumerate(sends)]
    cross, *got = lax.optimization_barrier((crossed(cross), *got))
    for part in got:
        mine = mine + part.astype(F32)
    (input_grad,) = call(last_kernel, [field], info, own, core_one, cross)
    bits = 2
    while bits < n_tile:
        mine = mine.astype(BF16)
        mine = mine.astype(F32) + swapped(mine, "tile", bits).astype(F32)
        bits *= 2
    voxel_total = n_grp * n_tile * rows
    mine = mine[:, :half] * float(voxel_total) ** (-0.5)
    other = swapped(mine, "tile", 1)
    odd = tile % 2 == 1
    whole = jnp.concatenate(
        [jnp.where(odd, other, mine), jnp.where(odd, mine, other)], axis=1
    )
    return (result, input_grad, whole[0], whole[1])


def solution(mesh):
    in_specs = (
        P(("grp", "tile"), None),
        P(None, ("grp", "tile"), None),
        P(None, ("grp", "tile")),
        P(("grp", "tile")),
        P(),
        P(),
        P(("grp", "tile"), None),
    )
    out_specs = (P(("grp", "tile"), None), P(("grp", "tile"), None), P("grp", None), P("grp", None))
    return jax.shard_map(
        on_device, mesh=mesh, in_specs=in_specs, out_specs=out_specs, check_vma=False
    )
```

```python
import jax
import jax.numpy as jnp
from jax import lax
from jax.experimental import pallas as pl
from jax.experimental.pallas import tpu as pltpu
from jax.sharding import PartitionSpec as P

F32 = jnp.float32
BF16 = jnp.bfloat16
KINDS = 3
LIMIT = 28 * 1024 * 1024
NT = (((1,), (1,)), ((), ()))


def swapped(value, axis, bits):
    count = lax.axis_size(axis)
    return lax.ppermute(value, axis, [(i, i ^ bits) for i in range(count) if i ^ bits < count])


def crossed(value):
    groups, count = lax.axis_size("grp"), lax.axis_size("tile")
    pairs = []
    for i in range(groups * count):
        group, tile = divmod(i, count)
        other = ((tile + 1) ^ 1) - 1
        if 0 <= other < count:
            pairs.append((i, group * count + other))
        elif (group ^ 1) < groups:
            pairs.append((i, (group ^ 1) * count + tile))
    return lax.ppermute(value, ("grp", "tile"), pairs)


def sigmoid_terms(values):
    sigma = jax.nn.sigmoid(values)
    return values * sigma, sigma * (1.0 + values * (1.0 - sigma))


def halo_sides(odd, core, cross):
    return jnp.where(odd, cross, core), jnp.where(odd, core, cross)


def row_mask(rows, blk, count):
    block = lax.broadcasted_iota(jnp.int32, (rows, 1), 0) // blk
    return (block < count).astype(F32)


def pack_kernel(info, features, source_rows, codes, entries, core_out, cross_out):
    offsets, _, blk = source_rows.shape
    per = offsets // KINDS
    odd, count = info[0] == 1, info[1]
    coded = []
    for j in range(2):
        rows = source_rows[:, j, :]
        block = lax.rem(codes[:, j : j + 1], 2)
        live = (rows >= 0) & (count > j)
        coded.append(jnp.where(live, rows + blk * block, -1).astype(F32))
    first, second = coded
    both = count == 2
    entries[0] = first
    entries[1] = second
    head = jnp.where(info[3] == 0, -1.0, first)
    to_prev = jnp.concatenate([head[i * KINDS : i * KINDS + 1] for i in range(per)], axis=0)
    last = jnp.where(info[3] == 1, -1.0, jnp.where(both, second, first))
    to_next = jnp.concatenate([last[i * KINDS + 2 : i * KINDS + 3] for i in range(per)], axis=0)
    front, back = features[:blk, :], features[blk:, :]
    tail = jnp.where(both, back, front)
    pad = core_out.shape[0] - blk - per
    fill = jnp.full((pad, blk), -1.0, F32)
    to_prev = jnp.concatenate([to_prev, fill], axis=0).astype(BF16)
    to_next = jnp.concatenate([to_next, fill], axis=0).astype(BF16)
    core_out[:blk, :] = jnp.where(odd, front, tail)
    cross_out[:blk, :] = jnp.where(odd, tail, front)
    core_out[blk:, :] = jnp.where(odd, to_prev, to_next)
    cross_out[blk:, :] = jnp.where(odd, to_next, to_prev)


def targets_by_sources(columns, kind, per, index, blk):
    lane = lax.broadcasted_iota(jnp.int32, (blk, blk), 1).astype(F32)
    halves = []
    for side in range(2):
        at = (kind * 2 + side) * per + index
        entry = jnp.broadcast_to(columns[:, at : at + 1], (blk, blk))
        halves.append(jnp.concatenate([entry, entry - blk], axis=0))
    wide = jnp.concatenate([lane, lane], axis=0)
    parts = [jnp.where(half == wide, 1.0, 0.0).astype(BF16) for half in halves]
    return jnp.concatenate(parts, axis=1)


def sources_by_targets(entries, kind, per, index, blk):
    sub = lax.broadcasted_iota(jnp.int32, (blk, 2 * blk), 0).astype(F32)
    parts = []
    for side in range(2):
        at = (kind * 2 + side) * per + index
        row = entries[at : at + 1, :]
        wide = jnp.concatenate([row, row - blk], axis=1)
        parts.append(jnp.where(wide == sub, 1.0, 0.0).astype(BF16))
    return jnp.concatenate(parts, axis=0)


def convolve(columns, sources, weights, picked):
    blk, channels = columns.shape[0], weights.shape[1]
    per = picked.shape[1] // channels // KINDS
    for kind in range(KINDS):
        for i in range(per):
            select = targets_by_sources(columns, kind, per, i, blk)
            got = jnp.dot(select, sources[kind], preferred_element_type=F32)
            at = (i * KINDS + kind) * channels
            picked[:, at : at + channels] = got.astype(BF16)
    return jnp.dot(picked[...], weights[...], preferred_element_type=F32)


def pull_back(entries, grads, weights, sources, pulled, wgrad):
    blk, channels = entries.shape[1], grads.shape[1]
    per = pulled.shape[1] // channels // KINDS
    sums = []
    for kind in range(KINDS):
        base = kind * per * channels
        for i in range(per):
            select = sources_by_targets(entries, kind, per, i, blk)
            got = jnp.dot(select, grads, preferred_element_type=F32)
            at = base + i * channels
            pulled[:, at : at + channels] = got.astype(BF16)
        held = pulled[:, base : base + per * channels]
        wide = jnp.concatenate(
            [
                weights[(i * KINDS + kind) * channels : (i * KINDS + kind + 1) * channels, :]
                for i in range(per)
            ],
            axis=1,
        )
        sums.append(lax.dot_general(held, wide, NT, preferred_element_type=F32))
        turned = sources[kind].T
        terms = jnp.dot(turned, held, preferred_element_type=F32)
        for i in range(per):
            at = (i * KINDS + kind) * channels
            wgrad[at : at + channels, :] = terms[:, i * channels : (i + 1) * channels]
    return sums


def split_sums(sums, both, blk):
    low, mid, high = sums
    first = mid[:blk] + jnp.where(both, high[blk:], 0.0)
    second = mid[blk:] + low[blk:]
    return jnp.concatenate([first, second], axis=0), low[:blk], high[:blk]


def halves_out(odd_bit, wgrad, keep, send, at):
    shards, slot, _ = keep.shape
    rows = wgrad.shape[0] // shards // 2
    for s in range(shards):
        mine = pl.ds(s * 2 * rows + odd_bit * rows, rows)
        other = pl.ds(s * 2 * rows + (1 - odd_bit) * rows, rows)
        keep[s, :rows, :] = wgrad[mine, :]
        start = at + s * slot
        send[start : start + rows, :] = wgrad[other, :].astype(BF16)


def first_kernel(
    info, local, features, core_in, cross_in, weights,
    entries, halo, hidden, slope, core_out, cross_out, picked,
):
    blk = features.shape[0] // 2
    per = local.shape[1] // KINDS
    odd, count = info[0] == 1, info[1]
    both = count == 2
    from_next, from_prev = halo_sides(odd, core_in[...].astype(F32), cross_in[...].astype(F32))
    first, second = local[0], local[1]

    def of_kind(values, kind):
        return [values[i * KINDS + kind : i * KINDS + kind + 1] for i in range(per)]

    rows = [from_next[blk : blk + per]]
    rows += of_kind(second, 0) + of_kind(first, 1) + of_kind(second, 1)
    rows += [from_prev[blk : blk + per]]
    rows += of_kind(jnp.where(both, first, -1.0), 2)
    table = jnp.concatenate(rows, axis=0)
    entries[...] = table
    spare = -table.shape[0] % 8
    table = jnp.concatenate([table, jnp.zeros((spare, blk), F32)], axis=0)
    columns = table.T
    after, before = from_next[:blk].astype(BF16), from_prev[:blk].astype(BF16)
    halo[0] = after
    halo[1] = before
    front, back = features[:blk, :], features[blk:, :]
    sources = [
        jnp.concatenate([after, back], axis=0),
        features[...],
        jnp.concatenate([before, front], axis=0),
    ]
    pre = convolve(columns, sources, weights, picked)
    mask = row_mask(2 * blk, blk, count)
    value, grad = sigmoid_terms(pre)
    field = (value * mask).astype(BF16)
    hidden[...] = field
    slope[...] = grad * mask
    head = field[:blk]
    tail = jnp.where(both, field[blk:], head)
    core_out[...] = jnp.where(odd, head, tail)
    cross_out[...] = jnp.where(odd, tail, head)


def exchange_sides(odd, to_next, to_prev):
    return jnp.where(odd, to_prev, to_next), jnp.where(odd, to_next, to_prev)


def second_kernel(
    info, entries, features, hidden, core_in, cross_in, weights, cotangent,
    result, grads_out, own_out, keep, core_out, cross_out, picked, pulled, wgrad,
):
    blk = features.shape[0] // 2
    odd, count = info[0] == 1, info[1]
    both = count == 2
    after, before = halo_sides(odd, core_in[...], cross_in[...])
    front, back = hidden[:blk, :], hidden[blk:, :]
    sources = [
        jnp.concatenate([after, back], axis=0),
        hidden[...],
        jnp.concatenate([before, front], axis=0),
    ]
    table = entries[...]
    spare = -table.shape[0] % 8
    columns = jnp.concatenate([table, jnp.zeros((spare, blk), F32)], axis=0).T
    total = convolve(columns, sources, weights, picked) + features[...].astype(F32)
    mask = row_mask(2 * blk, blk, count)
    value, grad = sigmoid_terms(total)
    result[...] = (value * mask).astype(BF16)
    grads = (cotangent[...].astype(F32) * grad * mask).astype(BF16)
    grads_out[...] = grads
    sums = pull_back(entries, grads, weights, sources, pulled, wgrad)
    own, to_next, to_prev = split_sums(sums, both, blk)
    own_out[...] = own
    core, cross = exchange_sides(odd, to_next, to_prev)
    core_out[:blk, :] = core.astype(BF16)
    cross_out[...] = cross.astype(BF16)
    halves_out(info[0], wgrad, keep, core_out, blk)


def joined(own, odd, both, core_in, cross_in, blk):
    from_next, from_prev = halo_sides(odd, core_in, cross_in)
    first = own[:blk] + from_prev + jnp.where(both, 0.0, from_next)
    second = own[blk:] + jnp.where(both, from_next, 0.0)
    return jnp.concatenate([first, second], axis=0)


def third_kernel(
    info, entries, features, halo, own, core_in, cross_in, slope, grads_in, weights,
    own_out, keep, core_out, cross_out, pulled, wgrad,
):
    blk = features.shape[0] // 2
    odd, both = info[0] == 1, info[1] == 2
    core, cross = core_in[:blk, :].astype(F32), cross_in[...].astype(F32)
    summed = joined(own[...], odd, both, core, cross, blk)
    grads = (summed * slope[...]).astype(BF16)
    sources = [
        jnp.concatenate([halo[0], features[blk:, :]], axis=0),
        features[...],
        jnp.concatenate([halo[1], features[:blk, :]], axis=0),
    ]
    sums = pull_back(entries, grads, weights, sources, pulled, wgrad)
    own_sum, to_next, to_prev = split_sums(sums, both, blk)
    own_out[...] = own_sum + grads_in[...].astype(F32)
    core, cross = exchange_sides(odd, to_next, to_prev)
    core_out[:blk, :] = core.astype(BF16)
    cross_out[...] = cross.astype(BF16)
    halves_out(info[0], wgrad, keep, core_out, blk)


def last_kernel(info, own, core_in, cross_in, input_grad):
    blk = own.shape[0] // 2
    odd, both = info[0] == 1, info[1] == 2
    core, cross = core_in[:blk, :].astype(F32), cross_in[...].astype(F32)
    input_grad[...] = joined(own[...], odd, both, core, cross, blk).astype(BF16)


def shards_kernel(info, keep, core, own, *sends):
    shards, slot, _ = keep.shape
    blk = core.shape[0] - shards * slot
    me = info[2]
    for d in range(shards):
        to = me ^ d
        at = pl.ds(pl.multiple_of(blk + to * slot, 16), slot)
        value = keep[to] + core[at, :].astype(F32)
        if d == 0:
            own[...] = value
        else:
            sends[d - 1][...] = value.astype(BF16)


def after(first, later):
    return lax.optimization_barrier((first, later))[1]


def added(value, others):
    value = value.astype(F32)
    for other in others:
        value = value + other.astype(F32)
    return value


def call(kernel, outs, *args, scratch=(), micros=1):
    specs = [pl.BlockSpec(memory_space=pltpu.SMEM)]
    specs += [pl.BlockSpec(memory_space=pltpu.VMEM)] * (len(args) - 1)
    return pl.pallas_call(
        kernel,
        out_shape=[jax.ShapeDtypeStruct(shape, kind) for shape, kind in outs],
        in_specs=specs,
        out_specs=[pl.BlockSpec(memory_space=pltpu.VMEM)] * len(outs),
        scratch_shapes=[pltpu.VMEM(shape, kind) for shape, kind in scratch],
        compiler_params=pltpu.CompilerParams(vmem_limit_bytes=LIMIT),
        cost_estimate=pl.CostEstimate(
            flops=micros * 10**9, bytes_accessed=micros * 3 * 10**6, transcendentals=0
        ),
    )(*args)


def on_device(
    features, source_rows, target_codes, block_count, weight_one, weight_two, out_cotangent
):
    offsets, blocks_dev, blk = source_rows.shape
    rows, channels = features.shape
    n_grp, n_tile = lax.axis_size("grp"), lax.axis_size("tile")
    per = offsets // KINDS
    tile = lax.axis_index("tile")
    end = jnp.where(tile == 0, 0, jnp.where(tile == n_tile - 1, 1, 2))
    info = jnp.stack([tile % 2, block_count[0], lax.axis_index("grp"), end]).astype(jnp.int32)
    flat_one = weight_one.reshape(offsets * channels, channels)
    flat_two = weight_two.reshape(offsets * channels, channels)
    packed = blk + per + (-per % 16)
    half = offsets * channels // n_grp // 2
    wide = (rows, offsets * channels)
    field, block = ((rows, channels), BF16), ((blk, channels), BF16)
    summed = ((rows, channels), F32)
    slot = half + (-half % 16)
    keep_shape = ((n_grp, slot, channels), F32)
    core_shape = ((blk + n_grp * slot, channels), BF16)

    local, core, cross = call(
        pack_kernel,
        [((2, offsets, blk), F32), ((packed, channels), BF16), ((packed, channels), BF16)],
        info, features, source_rows, target_codes,
        micros=3,
    )
    cross, core = crossed(cross), swapped(core, "tile", 1)
    entries, halo, hidden, slope, core, cross = call(
        first_kernel,
        [((2 * offsets, blk), F32), ((2, blk, channels), BF16), field, summed, block, block],
        info, local, features, core, cross, flat_one,
        scratch=[(wide, BF16)],
        micros=3,
    )
    cross, core = crossed(cross), swapped(core, "tile", 1)
    result, grad_sum, own, keep_two, core_two, cross = call(
        second_kernel,
        [field, field, summed, keep_shape, core_shape, block],
        info, entries, features, hidden, core, cross, flat_two, out_cotangent,
        scratch=[(wide, BF16), (wide, BF16), ((offsets * channels, channels), F32)],
        micros=5,
    )
    cross, core_two = crossed(cross), swapped(core_two, "tile", 1)
    shard = (slot, channels)
    shards = [(shard, F32)] + [(shard, BF16)] * (n_grp - 1)
    mine_two, *sends_two = call(shards_kernel, shards, info, keep_two, core_two)
    got_two = [swapped(send, "grp", d + 1) for d, send in enumerate(sends_two)]
    own = after(sends_two[-1], own)
    own, keep_one, core_one, cross = call(
        third_kernel,
        [summed, keep_shape, core_shape, block],
        info, entries, features, halo, own, core_two, cross, slope, grad_sum, flat_one,
        scratch=[(wide, BF16), ((offsets * channels, channels), F32)],
        micros=3,
    )
    core_one = swapped(core_one, "tile", 1)
    mine_one, *sends_one = call(shards_kernel, shards, info, keep_one, core_one)
    got_one = [swapped(send, "grp", d + 1) for d, send in enumerate(sends_one)]
    cross = crossed(after(sends_one[-1], cross))
    got_two = [after(cross, got) for got in got_two]
    two = added(mine_two, got_two).astype(BF16)
    steps = [1 << b for b in range(1, (n_tile - 1).bit_length())]
    other_two = swapped(two, "tile", steps[0])
    one = added(mine_one, got_one).astype(BF16)
    one = after(cross, one)
    (input_grad,) = call(last_kernel, [field], info, own, core_one, cross)
    for at, bits in enumerate(steps):
        other_one = swapped(one, "tile", bits)
        two = added(two, [other_two])
        if at + 1 < len(steps):
            two = after(one, two.astype(BF16))
            other_two = swapped(two, "tile", steps[at + 1])
            one = added(one, [other_one]).astype(BF16)
        else:
            one = added(one, [other_one])
    voxel_total = n_grp * n_tile * rows
    scale = float(voxel_total) ** (-0.5)
    odd = tile % 2 == 1
    outs = []
    for half_sum in (one, two):
        half_sum = half_sum[:half] * scale
        other = swapped(half_sum, "tile", 1)
        outs.append(
            jnp.concatenate(
                [jnp.where(odd, other, half_sum), jnp.where(odd, half_sum, other)], axis=0
            )
        )
    return (result, input_grad, outs[0], outs[1])


def solution(mesh):
    in_specs = (
        P(("grp", "tile"), None),
        P(None, ("grp", "tile"), None),
        P(None, ("grp", "tile")),
        P(("grp", "tile")),
        P(),
        P(),
        P(("grp", "tile"), None),
    )
    out_specs = (P(("grp", "tile"), None), P(("grp", "tile"), None), P("grp", None), P("grp", None))
    return jax.shard_map(
        on_device, mesh=mesh, in_specs=in_specs, out_specs=out_specs, check_vma=False
    )
```

```python
import jax
import jax.numpy as jnp
from jax import lax
from jax.experimental import pallas as pl
from jax.experimental.pallas import tpu as pltpu
from jax.sharding import PartitionSpec as P

F32 = jnp.float32
BF16 = jnp.bfloat16
KINDS = 3
LIMIT = 28 * 1024 * 1024
NT = (((1,), (1,)), ((), ()))


def swapped(value, axis, bits):
    count = lax.axis_size(axis)
    return lax.ppermute(value, axis, [(i, i ^ bits) for i in range(count) if i ^ bits < count])


def crossed(value):
    groups, count = lax.axis_size("grp"), lax.axis_size("tile")
    pairs = []
    for i in range(groups * count):
        group, tile = divmod(i, count)
        other = ((tile + 1) ^ 1) - 1
        if 0 <= other < count:
            pairs.append((i, group * count + other))
        elif (group ^ 1) < groups:
            pairs.append((i, (group ^ 1) * count + tile))
    return lax.ppermute(value, ("grp", "tile"), pairs)


def sigmoid_terms(values):
    sigma = jax.nn.sigmoid(values)
    return values * sigma, sigma * (1.0 + values * (1.0 - sigma))


def place():
    tile = lax.axis_index("tile")
    return tile % 2 == 1, tile > 0, tile < lax.axis_size("tile") - 1


def halo_sides(odd, core, cross):
    return jnp.where(odd, cross, core), jnp.where(odd, core, cross)


def exchange_sides(odd, to_next, to_prev):
    return jnp.where(odd, to_prev, to_next), jnp.where(odd, to_next, to_prev)


def row_mask(rows, blk, count):
    block = lax.broadcasted_iota(jnp.int32, (rows, 1), 0) // blk
    return (block < count).astype(F32)


def of_kind(values, kind):
    return [values[i : i + 1] for i in range(kind, values.shape[0], KINDS)]


def stacked(rows, blk, fill):
    spare = -len(rows) % 8
    if spare:
        rows = rows + [jnp.full((spare, blk), fill, F32)]
    return jnp.concatenate(rows, axis=0)


def pack_kernel(count_ref, features, source_rows, codes, near, core_out, cross_out):
    offsets, _, blk = source_rows.shape
    per = offsets // KINDS
    count = count_ref[0]
    both = count == 2
    odd, has_prev, has_next = place()
    diagonal = lax.broadcasted_iota(jnp.int32, (offsets, offsets), 0) == lax.broadcasted_iota(
        jnp.int32, (offsets, offsets), 1
    )
    coded = []
    for j in range(2):
        rows = source_rows[:, j, :]
        block = lax.rem(codes[j : j + 1, :], 2).astype(F32)
        block = jnp.sum(jnp.where(diagonal, block, 0.0), axis=1, keepdims=True)
        live = (rows >= 0) & (count > j)
        coded.append(jnp.where(live, rows.astype(F32) + blk * block, -1.0))
    first, second = coded
    inner = jnp.where(both, first, -1.0)
    rows = of_kind(second, 0) + of_kind(first, 1) + of_kind(second, 1) + of_kind(inner, 2)
    near[...] = stacked(rows, blk, -1.0)
    to_prev = of_kind(jnp.where(has_prev, first, -1.0), 0)
    last = jnp.where(both, second, first)
    to_next = of_kind(jnp.where(has_next, last, -1.0), 2)
    pad = core_out.shape[0] - blk - per
    fill = [jnp.full((pad, blk), -1.0, F32)]
    to_prev = jnp.concatenate(to_prev + fill, axis=0).astype(BF16)
    to_next = jnp.concatenate(to_next + fill, axis=0).astype(BF16)
    front, back = features[:blk, :], features[blk:, :]
    tail = jnp.where(both, back, front)
    core_out[:blk, :], cross_out[:blk, :] = exchange_sides(odd, tail, front)
    core_out[blk:, :], cross_out[blk:, :] = exchange_sides(odd, to_next, to_prev)


def by_targets(columns, at, blk):
    lane = lax.broadcasted_iota(jnp.int32, (blk, blk), 1).astype(F32).astype(BF16)
    one, zero = jnp.ones((blk, blk), BF16), jnp.zeros((blk, blk), BF16)
    entry = jnp.broadcast_to(columns[:, at : at + 1], (blk, blk)).astype(BF16)
    halves = [jnp.where(entry == lane + b * blk, one, zero) for b in range(2)]
    return jnp.concatenate(halves, axis=0)


def by_sources(entries, at, blk):
    sub = lax.broadcasted_iota(jnp.int32, (blk, blk), 0).astype(F32).astype(BF16)
    one, zero = jnp.ones((blk, blk), BF16), jnp.zeros((blk, blk), BF16)
    entry = jnp.broadcast_to(entries[at : at + 1, :], (blk, blk)).astype(BF16)
    halves = [jnp.where(entry == sub + b * blk, one, zero) for b in range(2)]
    return jnp.concatenate(halves, axis=1)


def weights_of(weights, kind, per, axis):
    channels = weights.shape[1]
    parts = []
    for i in range(per):
        at = (i * KINDS + kind) * channels
        parts.append(weights[at : at + channels, :])
    return jnp.concatenate(parts, axis=axis)


def middle_part(pairs, source, weights, picked):
    per, channels = pairs.shape[0], weights.shape[1]
    for i in range(per):
        got = jnp.dot(pairs[i], source, preferred_element_type=F32)
        picked[:, i * channels : (i + 1) * channels] = got.astype(BF16)
    wide = weights_of(weights, 1, per, 0)
    return jnp.dot(picked[...], wide, preferred_element_type=F32)


def outer_part(far, singles, sources, weights, picked):
    per, channels = singles.shape[0] // 2, weights.shape[1]
    for side, source in enumerate(sources):
        for i in range(per):
            at = side * per + i
            select = jnp.concatenate([far[at], singles[at]], axis=1)
            got = jnp.dot(select, source, preferred_element_type=F32)
            picked[:, at * channels : (at + 1) * channels] = got.astype(BF16)
    wide = jnp.concatenate([weights_of(weights, kind, per, 0) for kind in (0, 2)], axis=0)
    return jnp.dot(picked[...], wide, preferred_element_type=F32)


def local_kernel(
    near, features, weights, pairs, singles, pairs_turned, singles_turned, part, picked
):
    blk = near.shape[1]
    per = pairs.shape[0]
    columns = near[...].T
    for i in range(per):
        at, to = per + i, 2 * per + i
        pairs[i, :, :blk] = by_targets(columns, at, blk)
        pairs[i, :, blk:] = by_targets(columns, to, blk)
        pairs_turned[i, :blk, :] = by_sources(near, at, blk)
        pairs_turned[i, blk:, :] = by_sources(near, to, blk)
    part[...] = middle_part(pairs, features[...], weights, picked)
    for i in range(per):
        for side, at in ((0, i), (1, 3 * per + i)):
            singles[side * per + i] = by_targets(columns, at, blk)
            singles_turned[side * per + i] = by_sources(near, at, blk)


def pull_back(far_turned, pairs_turned, singles_turned, grads, weights, sources, pulled, wgrad):
    per, channels = pairs_turned.shape[0], grads.shape[1]
    sums = []
    for kind in range(KINDS):
        base = kind * per * channels
        for i in range(per):
            if kind == 1:
                select = pairs_turned[i]
            else:
                side = (kind // 2) * per + i
                select = jnp.concatenate([far_turned[side], singles_turned[side]], axis=0)
            got = jnp.dot(select, grads, preferred_element_type=F32)
            at = base + i * channels
            pulled[:, at : at + channels] = got.astype(BF16)
        held = pulled[:, base : base + per * channels]
        wide = weights_of(weights, kind, per, 1)
        sums.append(lax.dot_general(held, wide, NT, preferred_element_type=F32))
        terms = jnp.dot(sources[kind].T, held, preferred_element_type=F32)
        for i in range(per):
            at = (i * KINDS + kind) * channels
            wgrad[at : at + channels, :] = terms[:, i * channels : (i + 1) * channels]
    return sums


def split_sums(sums, both, blk):
    low, mid, high = sums
    first = mid[:blk] + jnp.where(both, high[blk:], 0.0)
    second = mid[blk:] + low[blk:]
    return jnp.concatenate([first, second], axis=0), low[:blk], high[:blk]


def halves_out(odd, wgrad, keep, send, at):
    shards, slot, _ = keep.shape
    rows = wgrad.shape[0] // shards // 2
    bit = odd.astype(jnp.int32)
    for s in range(shards):
        mine = pl.ds((s * 2 + bit) * rows, rows)
        other = pl.ds((s * 2 + 1 - bit) * rows, rows)
        keep[s, :rows, :] = wgrad[mine, :]
        start = at + s * slot
        send[start : start + rows, :] = wgrad[other, :].astype(BF16)


def first_kernel(
    count_ref, features, core_in, cross_in, singles, part, weights,
    entries, far, halo, hidden, slope, core_out, cross_out, picked,
):
    blk = features.shape[0] // 2
    per = singles.shape[0] // 2
    count = count_ref[0]
    odd, _, _ = place()
    from_next, from_prev = halo_sides(odd, core_in[...].astype(F32), cross_in[...].astype(F32))
    table = stacked([from_next[blk : blk + per], from_prev[blk : blk + per]], blk, -1.0)
    entries[...] = table
    columns = table.T
    for at in range(2 * per):
        far[at] = by_targets(columns, at, blk)
    after, before = from_next[:blk].astype(BF16), from_prev[:blk].astype(BF16)
    halo[0] = after
    halo[1] = before
    front, back = features[:blk, :], features[blk:, :]
    sources = [
        jnp.concatenate([after, back], axis=0),
        jnp.concatenate([before, front], axis=0),
    ]
    pre = part[...] + outer_part(far, singles, sources, weights, picked)
    mask = row_mask(2 * blk, blk, count)
    value, grad = sigmoid_terms(pre)
    field = (value * mask).astype(BF16)
    hidden[...] = field
    slope[...] = grad * mask
    head = field[:blk]
    tail = jnp.where(count == 2, field[blk:], head)
    core_out[...], cross_out[...] = exchange_sides(odd, tail, head)


def middle_kernel(hidden, pairs, entries, weights, part, far_turned, picked):
    part[...] = middle_part(pairs, hidden[...], weights, picked)
    for at in range(far_turned.shape[0]):
        far_turned[at] = by_sources(entries, at, entries.shape[1])


def second_kernel(
    count_ref, features, hidden, core_in, cross_in, far, singles, part, weights, cotangent,
    far_turned, pairs_turned, singles_turned,
    result, grads_out, own_out, keep, core_out, cross_out, picked, pulled, wgrad,
):
    blk = features.shape[0] // 2
    count = count_ref[0]
    both = count == 2
    odd, _, _ = place()
    after, before = halo_sides(odd, core_in[...], cross_in[...])
    front, back = hidden[:blk, :], hidden[blk:, :]
    low = jnp.concatenate([after, back], axis=0)
    high = jnp.concatenate([before, front], axis=0)
    total = part[...] + outer_part(far, singles, [low, high], weights, picked)
    total = total + features[...].astype(F32)
    mask = row_mask(2 * blk, blk, count)
    value, grad = sigmoid_terms(total)
    result[...] = (value * mask).astype(BF16)
    grads = (cotangent[...].astype(F32) * grad * mask).astype(BF16)
    grads_out[...] = grads
    sources = [low, hidden[...], high]
    sums = pull_back(
        far_turned, pairs_turned, singles_turned, grads, weights, sources, pulled, wgrad
    )
    own, to_next, to_prev = split_sums(sums, both, blk)
    own_out[...] = own
    core, cross = exchange_sides(odd, to_next, to_prev)
    core_out[:blk, :] = core.astype(BF16)
    cross_out[...] = cross.astype(BF16)
    halves_out(odd, wgrad, keep, core_out, blk)


def joined(own, odd, both, core_in, cross_in, blk):
    from_next, from_prev = halo_sides(odd, core_in, cross_in)
    first = own[:blk] + from_prev + jnp.where(both, 0.0, from_next)
    second = own[blk:] + jnp.where(both, from_next, 0.0)
    return jnp.concatenate([first, second], axis=0)


def third_kernel(
    count_ref, features, halo, own, core_in, cross_in, slope, grads_in, weights,
    far_turned, pairs_turned, singles_turned,
    own_out, keep, core_out, cross_out, pulled, wgrad,
):
    blk = features.shape[0] // 2
    both = count_ref[0] == 2
    odd, _, _ = place()
    core, cross = core_in[:blk, :].astype(F32), cross_in[...].astype(F32)
    summed = joined(own[...], odd, both, core, cross, blk)
    grads = (summed * slope[...]).astype(BF16)
    sources = [
        jnp.concatenate([halo[0], features[blk:, :]], axis=0),
        features[...],
        jnp.concatenate([halo[1], features[:blk, :]], axis=0),
    ]
    sums = pull_back(
        far_turned, pairs_turned, singles_turned, grads, weights, sources, pulled, wgrad
    )
    own_sum, to_next, to_prev = split_sums(sums, both, blk)
    own_out[...] = own_sum + grads_in[...].astype(F32)
    core, cross = exchange_sides(odd, to_next, to_prev)
    core_out[:blk, :] = core.astype(BF16)
    cross_out[...] = cross.astype(BF16)
    halves_out(odd, wgrad, keep, core_out, blk)


def last_kernel(count_ref, own, core_in, cross_in, input_grad):
    blk = own.shape[0] // 2
    both = count_ref[0] == 2
    odd, _, _ = place()
    core, cross = core_in[:blk, :].astype(F32), cross_in[...].astype(F32)
    input_grad[...] = joined(own[...], odd, both, core, cross, blk).astype(BF16)


def shards_kernel(keep, core, own, *sends):
    shards, slot, _ = keep.shape
    blk = core.shape[0] - shards * slot
    me = lax.axis_index("grp")
    for d in range(shards):
        to = me ^ d
        at = pl.ds(pl.multiple_of(blk + to * slot, 16), slot)
        value = keep[to] + core[at, :].astype(F32)
        if d == 0:
            own[...] = value
        else:
            sends[d - 1][...] = value.astype(BF16)


def after(first, later):
    return lax.optimization_barrier((first, later))[1]


def added(value, others):
    value = value.astype(F32)
    for other in others:
        value = value + other.astype(F32)
    return value


def call(kernel, outs, *args, scratch=(), micros=1):
    vmem, smem = pl.BlockSpec(memory_space=pltpu.VMEM), pl.BlockSpec(memory_space=pltpu.SMEM)
    return pl.pallas_call(
        kernel,
        out_shape=[jax.ShapeDtypeStruct(shape, kind) for shape, kind in outs],
        in_specs=[smem if arg.shape == (1,) else vmem for arg in args],
        out_specs=[vmem] * len(outs),
        scratch_shapes=[pltpu.VMEM(shape, kind) for shape, kind in scratch],
        compiler_params=pltpu.CompilerParams(vmem_limit_bytes=LIMIT),
        cost_estimate=pl.CostEstimate(
            flops=micros * 10**9, bytes_accessed=micros * 3 * 10**6, transcendentals=0
        ),
    )(*args)


def on_device(
    features, source_rows, target_codes, block_count, weight_one, weight_two, out_cotangent
):
    offsets, _, blk = source_rows.shape
    rows, channels = features.shape
    n_grp, n_tile = lax.axis_size("grp"), lax.axis_size("tile")
    per = offsets // KINDS
    flat_one = weight_one.reshape(offsets * channels, channels)
    flat_two = weight_two.reshape(offsets * channels, channels)
    packed = blk + per + (-per % 16)
    half = offsets * channels // n_grp // 2
    slot = half + (-half % 16)
    field, block = ((rows, channels), BF16), ((blk, channels), BF16)
    summed = ((rows, channels), F32)
    keep_shape = ((n_grp, slot, channels), F32)
    core_shape = ((blk + n_grp * slot, channels), BF16)
    pairs_shape = ((per, 2 * blk, 2 * blk), BF16)
    single_shape, turned_shape = ((2 * per, 2 * blk, blk), BF16), ((2 * per, blk, 2 * blk), BF16)
    inner, outer = ((rows, per * channels), BF16), ((rows, 2 * per * channels), BF16)
    pulled = ((rows, offsets * channels), BF16)
    wgrad = ((offsets * channels, channels), F32)
    count = block_count

    near, core, cross = call(
        pack_kernel,
        [((4 * per + (-4 * per % 8), blk), F32), ((packed, channels), BF16), ((packed, channels), BF16)],
        count, features, source_rows, target_codes.T,
        micros=3,
    )
    cross, core = crossed(cross), swapped(core, "tile", 1)
    pairs, singles, pairs_turned, singles_turned, part = call(
        local_kernel,
        [pairs_shape, single_shape, pairs_shape, turned_shape, summed],
        near, features, flat_one,
        scratch=[inner],
        micros=2,
    )
    entries, far, halo, hidden, slope, core, cross = call(
        first_kernel,
        [
            ((2 * per + (-2 * per % 8), blk), F32), single_shape, ((2, blk, channels), BF16),
            field, summed, block, block,
        ],
        count, features, core, cross, singles, part, flat_one,
        scratch=[outer],
        micros=2,
    )
    cross, core = crossed(cross), swapped(core, "tile", 1)
    part, far_turned = call(
        middle_kernel,
        [summed, turned_shape],
        hidden, pairs, entries, flat_two,
        scratch=[inner],
        micros=1,
    )
    result, grad_sum, own, keep_two, core_two, cross = call(
        second_kernel,
        [field, field, summed, keep_shape, core_shape, block],
        count, features, hidden, core, cross, far, singles, part, flat_two, out_cotangent,
        far_turned, pairs_turned, singles_turned,
        scratch=[outer, pulled, wgrad],
        micros=4,
    )
    cross, core_two = crossed(cross), swapped(core_two, "tile", 1)
    shard = (slot, channels)
    shards = [(shard, F32)] + [(shard, BF16)] * (n_grp - 1)
    mine_two, *sends_two = call(shards_kernel, shards, keep_two, core_two)
    got_two = [swapped(send, "grp", d + 1) for d, send in enumerate(sends_two)]
    own = after(sends_two[-1], own)
    own, keep_one, core_one, cross = call(
        third_kernel,
        [summed, keep_shape, core_shape, block],
        count, features, halo, own, core_two, cross, slope, grad_sum, flat_one,
        far_turned, pairs_turned, singles_turned,
        scratch=[pulled, wgrad],
        micros=3,
    )
    core_one = swapped(core_one, "tile", 1)
    mine_one, *sends_one = call(shards_kernel, shards, keep_one, core_one)
    got_one = [swapped(send, "grp", d + 1) for d, send in enumerate(sends_one)]
    cross = crossed(after(sends_one[-1], cross))
    got_two = [after(cross, got) for got in got_two]
    two = added(mine_two, got_two).astype(BF16)
    steps = [1 << b for b in range(1, (n_tile - 1).bit_length())]
    other_two = swapped(two, "tile", steps[0])
    one = added(mine_one, got_one).astype(BF16)
    one = after(cross, one)
    (input_grad,) = call(last_kernel, [field], count, own, core_one, cross)
    for at, bits in enumerate(steps):
        other_one = swapped(one, "tile", bits)
        two = added(two, [other_two])
        if at + 1 < len(steps):
            two = after(one, two.astype(BF16))
            other_two = swapped(two, "tile", steps[at + 1])
            one = added(one, [other_one]).astype(BF16)
        else:
            one = added(one, [other_one])
    voxel_total = n_grp * n_tile * rows
    scale = float(voxel_total) ** (-0.5)
    odd = lax.axis_index("tile") % 2 == 1
    outs = []
    for half_sum in (one, two):
        half_sum = half_sum[:half] * scale
        other = swapped(half_sum, "tile", 1)
        outs.append(
            jnp.concatenate(
                [jnp.where(odd, other, half_sum), jnp.where(odd, half_sum, other)], axis=0
            )
        )
    return (result, input_grad, outs[0], outs[1])


def solution(mesh):
    in_specs = (
        P(("grp", "tile"), None),
        P(None, ("grp", "tile"), None),
        P(None, ("grp", "tile")),
        P(("grp", "tile")),
        P(),
        P(),
        P(("grp", "tile"), None),
    )
    out_specs = (P(("grp", "tile"), None), P(("grp", "tile"), None), P("grp", None), P("grp", None))
    return jax.shard_map(
        on_device, mesh=mesh, in_specs=in_specs, out_specs=out_specs, check_vma=False
    )
```

```python
import jax
import jax.numpy as jnp
from jax import lax
from jax.experimental import pallas as pl
from jax.experimental.pallas import tpu as pltpu
from jax.sharding import PartitionSpec as P

F32 = jnp.float32
BF16 = jnp.bfloat16
KINDS = 3
LIMIT = 28 * 1024 * 1024
NT = (((1,), (1,)), ((), ()))


def swapped(value, axis, bits):
    count = lax.axis_size(axis)
    return lax.ppermute(value, axis, [(i, i ^ bits) for i in range(count) if i ^ bits < count])


def crossed(value):
    groups, count = lax.axis_size("grp"), lax.axis_size("tile")
    pairs = []
    for i in range(groups * count):
        group, tile = divmod(i, count)
        other = ((tile + 1) ^ 1) - 1
        if 0 <= other < count:
            pairs.append((i, group * count + other))
        elif (group ^ 1) < groups:
            pairs.append((i, (group ^ 1) * count + tile))
    return lax.ppermute(value, ("grp", "tile"), pairs)


def sigmoid_terms(values):
    sigma = jax.nn.sigmoid(values)
    return values * sigma, sigma * (1.0 + values * (1.0 - sigma))


def place():
    tile = lax.axis_index("tile")
    return tile % 2 == 1, tile > 0, tile < lax.axis_size("tile") - 1


def halo_sides(odd, core, cross):
    return jnp.where(odd, cross, core), jnp.where(odd, core, cross)


def exchange_sides(odd, to_next, to_prev):
    return jnp.where(odd, to_prev, to_next), jnp.where(odd, to_next, to_prev)


def row_mask(rows, blk, count):
    block = lax.broadcasted_iota(jnp.int32, (rows, count.shape[1]), 0) // blk
    return (block < count).astype(F32)


def of_kind(values, kind):
    return [values[i : i + 1] for i in range(kind, values.shape[0], KINDS)]


def stacked(rows, blk, fill):
    spare = -len(rows) % 8
    if spare:
        rows = rows + [jnp.full((spare, blk), fill, F32)]
    return jnp.concatenate(rows, axis=0)


def pack_kernel(
    features_in, rows_in, codes_in, near, core_out, cross_out, count_out,
    features, source_rows, codes, done,
):
    copies = []
    for at, (source, target) in enumerate(
        [(rows_in, source_rows), (codes_in, codes), (features_in, features)]
    ):
        copies.append(pltpu.make_async_copy(source, target, done.at[at]))
        copies[-1].start()
    for copy in copies:
        copy.wait()
    offsets, _, blk = source_rows.shape
    per = offsets // KINDS
    count = jnp.where(codes[:1, KINDS - 1 : KINDS] // 2 == 2, 1, 2)
    count = jnp.broadcast_to(count, (1, blk))
    count_out[...] = jnp.broadcast_to(count, count_out.shape)
    both = count == 2
    odd, has_prev, has_next = place()
    diagonal = lax.broadcasted_iota(jnp.int32, (offsets, offsets), 0) == lax.broadcasted_iota(
        jnp.int32, (offsets, offsets), 1
    )
    coded = []
    for j in range(2):
        rows = source_rows[:, j, :]
        block = lax.rem(codes[j : j + 1, :], 2).astype(F32)
        block = jnp.sum(jnp.where(diagonal, block, 0.0), axis=1, keepdims=True)
        live = (rows >= 0) & (count > j)
        coded.append(jnp.where(live, rows.astype(F32) + blk * block, -1.0))
    first, second = coded
    inner = jnp.where(both, first, -1.0)
    rows = of_kind(second, 0) + of_kind(first, 1) + of_kind(second, 1) + of_kind(inner, 2)
    near[...] = stacked(rows, blk, -1.0)
    to_prev = of_kind(jnp.where(has_prev, first, -1.0), 0)
    last = jnp.where(both, second, first)
    to_next = of_kind(jnp.where(has_next, last, -1.0), 2)
    pad = core_out.shape[0] - blk - per
    fill = [jnp.full((pad, blk), -1.0, F32)]
    to_prev = jnp.concatenate(to_prev + fill, axis=0).astype(BF16)
    to_next = jnp.concatenate(to_next + fill, axis=0).astype(BF16)
    front, back = features[:blk, :], features[blk:, :]
    tail = jnp.where(both, back, front)
    core_out[:blk, :], cross_out[:blk, :] = exchange_sides(odd, tail, front)
    core_out[blk:, :], cross_out[blk:, :] = exchange_sides(odd, to_next, to_prev)


def by_targets(columns, at, blk):
    lane = lax.broadcasted_iota(jnp.int32, (blk, blk), 1).astype(F32).astype(BF16)
    one, zero = jnp.ones((blk, blk), BF16), jnp.zeros((blk, blk), BF16)
    entry = jnp.broadcast_to(columns[:, at : at + 1], (blk, blk)).astype(BF16)
    halves = [jnp.where(entry == lane + b * blk, one, zero) for b in range(2)]
    return jnp.concatenate(halves, axis=0)


def by_sources(entries, at, blk):
    sub = lax.broadcasted_iota(jnp.int32, (blk, blk), 0).astype(F32).astype(BF16)
    one, zero = jnp.ones((blk, blk), BF16), jnp.zeros((blk, blk), BF16)
    entry = jnp.broadcast_to(entries[at : at + 1, :], (blk, blk)).astype(BF16)
    halves = [jnp.where(entry == sub + b * blk, one, zero) for b in range(2)]
    return jnp.concatenate(halves, axis=1)


def weights_of(weights, kind, per, axis):
    channels = weights.shape[1]
    parts = []
    for i in range(per):
        at = (i * KINDS + kind) * channels
        parts.append(weights[at : at + channels, :])
    return jnp.concatenate(parts, axis=axis)


def middle_part(pairs, source, weights, picked):
    per, channels = pairs.shape[0], weights.shape[1]
    for i in range(per):
        got = jnp.dot(pairs[i], source, preferred_element_type=F32)
        picked[:, i * channels : (i + 1) * channels] = got.astype(BF16)
    wide = weights_of(weights, 1, per, 0)
    return jnp.dot(picked[...], wide, preferred_element_type=F32)


def outer_part(far, singles, sources, weights, picked):
    per, channels = singles.shape[0] // 2, weights.shape[1]
    for side, source in enumerate(sources):
        for i in range(per):
            at = side * per + i
            select = jnp.concatenate([far[at], singles[at]], axis=1)
            got = jnp.dot(select, source, preferred_element_type=F32)
            picked[:, at * channels : (at + 1) * channels] = got.astype(BF16)
    wide = jnp.concatenate([weights_of(weights, kind, per, 0) for kind in (0, 2)], axis=0)
    return jnp.dot(picked[...], wide, preferred_element_type=F32)


def local_kernel(
    near, features, weights, pairs, singles, pairs_turned, singles_turned, part, picked
):
    blk = near.shape[1]
    per = pairs.shape[0]
    columns = near[...].T
    for i in range(per):
        at, to = per + i, 2 * per + i
        pairs[i, :, :blk] = by_targets(columns, at, blk)
        pairs[i, :, blk:] = by_targets(columns, to, blk)
        pairs_turned[i, :blk, :] = by_sources(near, at, blk)
        pairs_turned[i, blk:, :] = by_sources(near, to, blk)
    part[...] = middle_part(pairs, features[...], weights, picked)
    for i in range(per):
        for side, at in ((0, i), (1, 3 * per + i)):
            singles[side * per + i] = by_targets(columns, at, blk)
            singles_turned[side * per + i] = by_sources(near, at, blk)


def pull_back(far_turned, pairs_turned, singles_turned, grads, weights, sources, pulled, wgrad):
    per, channels = pairs_turned.shape[0], grads.shape[1]
    sums = []
    for kind in range(KINDS):
        base = kind * per * channels
        for i in range(per):
            if kind == 1:
                select = pairs_turned[i]
            else:
                side = (kind // 2) * per + i
                select = jnp.concatenate([far_turned[side], singles_turned[side]], axis=0)
            got = jnp.dot(select, grads, preferred_element_type=F32)
            at = base + i * channels
            pulled[:, at : at + channels] = got.astype(BF16)
        held = pulled[:, base : base + per * channels]
        wide = weights_of(weights, kind, per, 1)
        sums.append(lax.dot_general(held, wide, NT, preferred_element_type=F32))
        terms = jnp.dot(sources[kind].T, held, preferred_element_type=F32)
        for i in range(per):
            at = (i * KINDS + kind) * channels
            wgrad[at : at + channels, :] = terms[:, i * channels : (i + 1) * channels]
    return sums


def split_sums(sums, both, blk):
    low, mid, high = sums
    first = mid[:blk] + jnp.where(both, high[blk:], 0.0)
    second = mid[blk:] + low[blk:]
    return jnp.concatenate([first, second], axis=0), low[:blk], high[:blk]


def halves_out(odd, wgrad, keep, send, at):
    shards, slot, _ = keep.shape
    rows = wgrad.shape[0] // shards // 2
    bit = odd.astype(jnp.int32)
    for s in range(shards):
        mine = pl.ds((s * 2 + bit) * rows, rows)
        other = pl.ds((s * 2 + 1 - bit) * rows, rows)
        keep[s, :rows, :] = wgrad[mine, :]
        start = at + s * slot
        send[start : start + rows, :] = wgrad[other, :].astype(BF16)


def first_kernel(
    count_ref, features, core_in, cross_in, singles, part, weights,
    entries, far, halo, hidden, slope, core_out, cross_out, picked,
):
    blk = features.shape[0] // 2
    per = singles.shape[0] // 2
    count = count_ref[:1, :]
    odd, _, _ = place()
    from_next, from_prev = halo_sides(odd, core_in[...].astype(F32), cross_in[...].astype(F32))
    table = stacked([from_next[blk : blk + per], from_prev[blk : blk + per]], blk, -1.0)
    entries[...] = table
    columns = table.T
    for at in range(2 * per):
        far[at] = by_targets(columns, at, blk)
    after, before = from_next[:blk].astype(BF16), from_prev[:blk].astype(BF16)
    halo[0] = after
    halo[1] = before
    front, back = features[:blk, :], features[blk:, :]
    sources = [
        jnp.concatenate([after, back], axis=0),
        jnp.concatenate([before, front], axis=0),
    ]
    pre = part[...] + outer_part(far, singles, sources, weights, picked)
    mask = row_mask(2 * blk, blk, count)
    value, grad = sigmoid_terms(pre)
    field = (value * mask).astype(BF16)
    hidden[...] = field
    slope[...] = grad * mask
    head = field[:blk]
    tail = jnp.where(count == 2, field[blk:], head)
    core_out[...], cross_out[...] = exchange_sides(odd, tail, head)


def middle_kernel(hidden, pairs, entries, weights, part, far_turned, picked):
    part[...] = middle_part(pairs, hidden[...], weights, picked)
    for at in range(far_turned.shape[0]):
        far_turned[at] = by_sources(entries, at, entries.shape[1])


def second_kernel(
    count_ref, features, hidden, core_in, cross_in, far, singles, part, weights, cotangent,
    far_turned, pairs_turned, singles_turned,
    result, grads_out, own_out, keep, core_out, cross_out, picked, pulled, wgrad,
):
    blk = features.shape[0] // 2
    count = count_ref[:1, :]
    both = count == 2
    odd, _, _ = place()
    after, before = halo_sides(odd, core_in[...], cross_in[...])
    front, back = hidden[:blk, :], hidden[blk:, :]
    low = jnp.concatenate([after, back], axis=0)
    high = jnp.concatenate([before, front], axis=0)
    total = part[...] + outer_part(far, singles, [low, high], weights, picked)
    total = total + features[...].astype(F32)
    mask = row_mask(2 * blk, blk, count)
    value, grad = sigmoid_terms(total)
    result[...] = (value * mask).astype(BF16)
    grads = (cotangent[...].astype(F32) * grad * mask).astype(BF16)
    grads_out[...] = grads
    sources = [low, hidden[...], high]
    sums = pull_back(
        far_turned, pairs_turned, singles_turned, grads, weights, sources, pulled, wgrad
    )
    own, to_next, to_prev = split_sums(sums, both, blk)
    own_out[...] = own
    core, cross = exchange_sides(odd, to_next, to_prev)
    core_out[:blk, :] = core.astype(BF16)
    cross_out[...] = cross.astype(BF16)
    halves_out(odd, wgrad, keep, core_out, blk)


def joined(own, odd, both, core_in, cross_in, blk):
    from_next, from_prev = halo_sides(odd, core_in, cross_in)
    first = own[:blk] + from_prev + jnp.where(both, 0.0, from_next)
    second = own[blk:] + jnp.where(both, from_next, 0.0)
    return jnp.concatenate([first, second], axis=0)


def third_kernel(
    count_ref, features, halo, own, core_in, cross_in, slope, grads_in, weights,
    far_turned, pairs_turned, singles_turned,
    own_out, keep, core_out, cross_out, pulled, wgrad,
):
    blk = features.shape[0] // 2
    both = count_ref[:1, :] == 2
    odd, _, _ = place()
    core, cross = core_in[:blk, :].astype(F32), cross_in[...].astype(F32)
    summed = joined(own[...], odd, both, core, cross, blk)
    grads = (summed * slope[...]).astype(BF16)
    sources = [
        jnp.concatenate([halo[0], features[blk:, :]], axis=0),
        features[...],
        jnp.concatenate([halo[1], features[:blk, :]], axis=0),
    ]
    sums = pull_back(
        far_turned, pairs_turned, singles_turned, grads, weights, sources, pulled, wgrad
    )
    own_sum, to_next, to_prev = split_sums(sums, both, blk)
    own_out[...] = own_sum + grads_in[...].astype(F32)
    core, cross = exchange_sides(odd, to_next, to_prev)
    core_out[:blk, :] = core.astype(BF16)
    cross_out[...] = cross.astype(BF16)
    halves_out(odd, wgrad, keep, core_out, blk)


def last_kernel(count_ref, own, core_in, cross_in, input_grad):
    blk = own.shape[0] // 2
    both = count_ref[:1, :] == 2
    odd, _, _ = place()
    core, cross = core_in[:blk, :].astype(F32), cross_in[...].astype(F32)
    input_grad[...] = joined(own[...], odd, both, core, cross, blk).astype(BF16)


def shards_kernel(keep, core, own, *sends):
    shards, slot, _ = keep.shape
    blk = core.shape[0] - shards * slot
    me = lax.axis_index("grp")
    for d in range(shards):
        to = me ^ d
        at = pl.ds(pl.multiple_of(blk + to * slot, 16), slot)
        value = keep[to] + core[at, :].astype(F32)
        if d == 0:
            own[...] = value
        else:
            sends[d - 1][...] = value.astype(BF16)


def after(first, later):
    return lax.optimization_barrier((first, later))[1]


def added(value, others):
    value = value.astype(F32)
    for other in others:
        value = value + other.astype(F32)
    return value


def call(kernel, outs, *args, scratch=(), micros=1, far=False):
    vmem = pl.BlockSpec(memory_space=pltpu.VMEM)
    return pl.pallas_call(
        kernel,
        out_shape=[jax.ShapeDtypeStruct(shape, kind) for shape, kind in outs],
        in_specs=[pl.BlockSpec(memory_space=pltpu.HBM if far else pltpu.VMEM)] * len(args),
        out_specs=[vmem] * len(outs),
        scratch_shapes=[pltpu.VMEM(*one) if isinstance(one, tuple) else one for one in scratch],
        compiler_params=pltpu.CompilerParams(vmem_limit_bytes=LIMIT),
        cost_estimate=pl.CostEstimate(
            flops=micros * 10**9, bytes_accessed=micros * 3 * 10**6, transcendentals=0
        ),
    )(*args)


def on_device(
    features, source_rows, target_codes, block_count, weight_one, weight_two, out_cotangent
):
    offsets, _, blk = source_rows.shape
    rows, channels = features.shape
    n_grp, n_tile = lax.axis_size("grp"), lax.axis_size("tile")
    per = offsets // KINDS
    flat_one = weight_one.reshape(offsets * channels, channels)
    flat_two = weight_two.reshape(offsets * channels, channels)
    packed = blk + per + (-per % 16)
    half = offsets * channels // n_grp // 2
    slot = half + (-half % 16)
    field, block = ((rows, channels), BF16), ((blk, channels), BF16)
    summed = ((rows, channels), F32)
    keep_shape = ((n_grp, slot, channels), F32)
    core_shape = ((blk + n_grp * slot, channels), BF16)
    pairs_shape = ((per, 2 * blk, 2 * blk), BF16)
    single_shape, turned_shape = ((2 * per, 2 * blk, blk), BF16), ((2 * per, blk, 2 * blk), BF16)
    inner, outer = ((rows, per * channels), BF16), ((rows, 2 * per * channels), BF16)
    pulled = ((rows, offsets * channels), BF16)
    wgrad = ((offsets * channels, channels), F32)

    near, core, cross, count = call(
        pack_kernel,
        [
            ((4 * per + (-4 * per % 8), blk), F32), ((packed, channels), BF16),
            ((packed, channels), BF16), ((8, channels), jnp.int32),
        ],
        *[
            pltpu.with_memory_space_constraint(value, pltpu.HBM)
            for value in (features, source_rows, target_codes.T)
        ],
        scratch=[
            pltpu.VMEM(features.shape, BF16), pltpu.VMEM(source_rows.shape, jnp.int32),
            pltpu.VMEM(target_codes.shape[::-1], jnp.int32),
            pltpu.SemaphoreType.DMA((3,)),
        ],
        micros=3,
        far=True,
    )
    cross, core = crossed(cross), swapped(core, "tile", 1)
    pairs, singles, pairs_turned, singles_turned, part = call(
        local_kernel,
        [pairs_shape, single_shape, pairs_shape, turned_shape, summed],
        near, features, flat_one,
        scratch=[inner],
        micros=2,
    )
    entries, far, halo, hidden, slope, core, cross = call(
        first_kernel,
        [
            ((2 * per + (-2 * per % 8), blk), F32), single_shape, ((2, blk, channels), BF16),
            field, summed, block, block,
        ],
        count, features, core, cross, singles, part, flat_one,
        scratch=[outer],
        micros=2,
    )
    cross, core = crossed(cross), swapped(core, "tile", 1)
    part, far_turned = call(
        middle_kernel,
        [summed, turned_shape],
        hidden, pairs, entries, flat_two,
        scratch=[inner],
        micros=1,
    )
    result, grad_sum, own, keep_two, core_two, cross = call(
        second_kernel,
        [field, field, summed, keep_shape, core_shape, block],
        count, features, hidden, core, cross, far, singles, part, flat_two, out_cotangent,
        far_turned, pairs_turned, singles_turned,
        scratch=[outer, pulled, wgrad],
        micros=4,
    )
    cross, core_two = crossed(cross), swapped(core_two, "tile", 1)
    shard = (slot, channels)
    shards = [(shard, F32)] + [(shard, BF16)] * (n_grp - 1)
    mine_two, *sends_two = call(shards_kernel, shards, keep_two, core_two)
    got_two = [swapped(send, "grp", d + 1) for d, send in enumerate(sends_two)]
    own = after(sends_two[-1], own)
    own, keep_one, core_one, cross = call(
        third_kernel,
        [summed, keep_shape, core_shape, block],
        count, features, halo, own, core_two, cross, slope, grad_sum, flat_one,
        far_turned, pairs_turned, singles_turned,
        scratch=[pulled, wgrad],
        micros=3,
    )
    core_one = swapped(core_one, "tile", 1)
    mine_one, *sends_one = call(shards_kernel, shards, keep_one, core_one)
    got_one = [swapped(send, "grp", d + 1) for d, send in enumerate(sends_one)]
    cross = crossed(after(sends_one[-1], cross))
    got_two = [after(cross, got) for got in got_two]
    two = added(mine_two, got_two).astype(BF16)
    steps = [1 << b for b in range(1, (n_tile - 1).bit_length())]
    other_two = swapped(two, "tile", steps[0])
    one = added(mine_one, got_one).astype(BF16)
    one = after(cross, one)
    (input_grad,) = call(last_kernel, [field], count, own, core_one, cross)
    for at, bits in enumerate(steps):
        other_one = swapped(one, "tile", bits)
        two = added(two, [other_two])
        if at + 1 < len(steps):
            two = after(one, two.astype(BF16))
            other_two = swapped(two, "tile", steps[at + 1])
            one = added(one, [other_one]).astype(BF16)
        else:
            one = added(one, [other_one])
    voxel_total = n_grp * n_tile * rows
    scale = float(voxel_total) ** (-0.5)
    odd = lax.axis_index("tile") % 2 == 1
    outs = []
    for half_sum in (one, two):
        half_sum = half_sum[:half] * scale
        other = swapped(half_sum, "tile", 1)
        outs.append(
            jnp.concatenate(
                [jnp.where(odd, other, half_sum), jnp.where(odd, half_sum, other)], axis=0
            )
        )
    return (result, input_grad, outs[0], outs[1])


def solution(mesh):
    in_specs = (
        P(("grp", "tile"), None),
        P(None, ("grp", "tile"), None),
        P(None, ("grp", "tile")),
        P(("grp", "tile")),
        P(),
        P(),
        P(("grp", "tile"), None),
    )
    out_specs = (P(("grp", "tile"), None), P(("grp", "tile"), None), P("grp", None), P("grp", None))
    return jax.shard_map(
        on_device, mesh=mesh, in_specs=in_specs, out_specs=out_specs, check_vma=False
    )
```

```python
import jax
import jax.numpy as jnp
from jax import lax
from jax.experimental import pallas as pl
from jax.experimental.pallas import tpu as pltpu
from jax.sharding import PartitionSpec as P

F32 = jnp.float32
BF16 = jnp.bfloat16
KINDS = 3
LIMIT = 28 * 1024 * 1024
NT = (((1,), (1,)), ((), ()))


def swapped(value, axis, bits):
    count = lax.axis_size(axis)
    return lax.ppermute(value, axis, [(i, i ^ bits) for i in range(count) if i ^ bits < count])


def crossed(value):
    groups, count = lax.axis_size("grp"), lax.axis_size("tile")
    pairs = []
    for i in range(groups * count):
        group, tile = divmod(i, count)
        other = ((tile + 1) ^ 1) - 1
        if 0 <= other < count:
            pairs.append((i, group * count + other))
        elif (group ^ 1) < groups:
            pairs.append((i, (group ^ 1) * count + tile))
    return lax.ppermute(value, ("grp", "tile"), pairs)


def sigmoid_terms(values):
    sigma = jax.nn.sigmoid(values)
    return values * sigma, sigma * (1.0 + values * (1.0 - sigma))


def place():
    tile = lax.axis_index("tile")
    return tile % 2 == 1, tile > 0, tile < lax.axis_size("tile") - 1


def halo_sides(odd, core, cross):
    return jnp.where(odd, cross, core), jnp.where(odd, core, cross)


def exchange_sides(odd, to_next, to_prev):
    return jnp.where(odd, to_prev, to_next), jnp.where(odd, to_next, to_prev)


def row_mask(rows, blk, count):
    block = lax.broadcasted_iota(jnp.int32, (rows, count.shape[1]), 0) // blk
    return (block < count).astype(F32)


def of_kind(values, kind):
    return [values[i : i + 1] for i in range(kind, values.shape[0], KINDS)]


def stacked(rows, blk, fill):
    spare = -len(rows) % 8
    if spare:
        rows = rows + [jnp.full((spare, blk), fill, F32)]
    return jnp.concatenate(rows, axis=0)


def pack_kernel(
    features_in, rows_in, codes_in, near, core_out, cross_out, count_out,
    features, source_rows, codes, done,
):
    copies = []
    for at, (source, target) in enumerate(
        [(rows_in, source_rows), (codes_in, codes), (features_in, features)]
    ):
        copies.append(pltpu.make_async_copy(source, target, done.at[at]))
        copies[-1].start()
    for copy in copies:
        copy.wait()
    offsets, _, blk = source_rows.shape
    per = offsets // KINDS
    count = jnp.where(codes[:1, KINDS - 1 : KINDS] // 2 == 2, 1, 2)
    count = jnp.broadcast_to(count, (1, blk))
    count_out[...] = jnp.broadcast_to(count, count_out.shape)
    both = count == 2
    odd, has_prev, has_next = place()
    diagonal = lax.broadcasted_iota(jnp.int32, (offsets, offsets), 0) == lax.broadcasted_iota(
        jnp.int32, (offsets, offsets), 1
    )
    coded = []
    for j in range(2):
        rows = source_rows[:, j, :]
        block = lax.rem(codes[j : j + 1, :], 2).astype(F32)
        block = jnp.sum(jnp.where(diagonal, block, 0.0), axis=1, keepdims=True)
        live = (rows >= 0) & (count > j)
        coded.append(jnp.where(live, rows.astype(F32) + blk * block, -1.0))
    first, second = coded
    inner = jnp.where(both, first, -1.0)
    rows = of_kind(second, 0) + of_kind(first, 1) + of_kind(second, 1) + of_kind(inner, 2)
    near[...] = stacked(rows, blk, -1.0)
    to_prev = of_kind(jnp.where(has_prev, first, -1.0), 0)
    last = jnp.where(both, second, first)
    to_next = of_kind(jnp.where(has_next, last, -1.0), 2)
    pad = core_out.shape[0] - blk - per
    fill = [jnp.full((pad, blk), -1.0, F32)]
    to_prev = jnp.concatenate(to_prev + fill, axis=0).astype(BF16)
    to_next = jnp.concatenate(to_next + fill, axis=0).astype(BF16)
    front, back = features[:blk, :], features[blk:, :]
    tail = jnp.where(both, back, front)
    core_out[:blk, :], cross_out[:blk, :] = exchange_sides(odd, tail, front)
    core_out[blk:, :], cross_out[blk:, :] = exchange_sides(odd, to_next, to_prev)


def by_targets(columns, at, blk):
    lane = lax.broadcasted_iota(jnp.int32, (blk, blk), 1).astype(F32).astype(BF16)
    one, zero = jnp.ones((blk, blk), BF16), jnp.zeros((blk, blk), BF16)
    entry = jnp.broadcast_to(columns[:, at : at + 1], (blk, blk)).astype(BF16)
    halves = [jnp.where(entry == lane + b * blk, one, zero) for b in range(2)]
    return jnp.concatenate(halves, axis=0)


def by_sources(entries, at, blk):
    sub = lax.broadcasted_iota(jnp.int32, (blk, blk), 0).astype(F32).astype(BF16)
    one, zero = jnp.ones((blk, blk), BF16), jnp.zeros((blk, blk), BF16)
    entry = jnp.broadcast_to(entries[at : at + 1, :], (blk, blk)).astype(BF16)
    halves = [jnp.where(entry == sub + b * blk, one, zero) for b in range(2)]
    return jnp.concatenate(halves, axis=1)


def weights_of(weights, kind, per, axis):
    channels = weights.shape[1]
    parts = []
    for i in range(per):
        at = (i * KINDS + kind) * channels
        parts.append(weights[at : at + channels, :])
    return jnp.concatenate(parts, axis=axis)


def middle_part(pairs, source, weights, picked):
    per, channels = pairs.shape[0], weights.shape[1]
    for i in range(per):
        got = jnp.dot(pairs[i], source, preferred_element_type=F32)
        picked[:, i * channels : (i + 1) * channels] = got.astype(BF16)
    wide = weights_of(weights, 1, per, 0)
    return jnp.dot(picked[...], wide, preferred_element_type=F32)


def outer_part(far, singles, sources, weights, picked):
    per, channels = singles.shape[0] // 2, weights.shape[1]
    for side, source in enumerate(sources):
        for i in range(per):
            at = side * per + i
            select = jnp.concatenate([far[at], singles[at]], axis=1)
            got = jnp.dot(select, source, preferred_element_type=F32)
            picked[:, at * channels : (at + 1) * channels] = got.astype(BF16)
    wide = jnp.concatenate([weights_of(weights, kind, per, 0) for kind in (0, 2)], axis=0)
    return jnp.dot(picked[...], wide, preferred_element_type=F32)


def local_kernel(
    near, features, weights, pairs, singles, pairs_turned, singles_turned, part, picked
):
    blk = near.shape[1]
    per = pairs.shape[0]
    columns = near[...].T
    for i in range(per):
        at, to = per + i, 2 * per + i
        pairs[i, :, :blk] = by_targets(columns, at, blk)
        pairs[i, :, blk:] = by_targets(columns, to, blk)
        pairs_turned[i, :blk, :] = by_sources(near, at, blk)
        pairs_turned[i, blk:, :] = by_sources(near, to, blk)
    part[...] = middle_part(pairs, features[...], weights, picked)
    for i in range(per):
        for side, at in ((0, i), (1, 3 * per + i)):
            singles[side * per + i] = by_targets(columns, at, blk)
            singles_turned[side * per + i] = by_sources(near, at, blk)


def pull(far_turned, pairs_turned, singles_turned, grads, pulled, kind):
    per, channels = pairs_turned.shape[0], grads.shape[1]
    for i in range(per):
        if kind == 1:
            select = pairs_turned[i]
        else:
            side = (kind // 2) * per + i
            select = jnp.concatenate([far_turned[side], singles_turned[side]], axis=0)
        got = jnp.dot(select, grads, preferred_element_type=F32)
        at = (kind * per + i) * channels
        pulled[:, at : at + channels] = got.astype(BF16)


def of_kind_in(pulled, kind):
    wide = pulled.shape[1] // KINDS
    return pulled[:, kind * wide : (kind + 1) * wide]


def source_sums(pulled, weights, kind):
    per = weights.shape[0] // weights.shape[1] // KINDS
    wide = weights_of(weights, kind, per, 1)
    return lax.dot_general(of_kind_in(pulled, kind), wide, NT, preferred_element_type=F32)


def weight_sums(pulled, source, wgrad, kind):
    channels = wgrad.shape[1]
    terms = jnp.dot(source.T, of_kind_in(pulled, kind), preferred_element_type=F32)
    for i in range(terms.shape[1] // channels):
        at = (i * KINDS + kind) * channels
        wgrad[at : at + channels, :] = terms[:, i * channels : (i + 1) * channels]


def split_sums(sums, both, blk):
    low, mid, high = sums
    first = mid[:blk] + jnp.where(both, high[blk:], 0.0)
    second = mid[blk:] + low[blk:]
    return jnp.concatenate([first, second], axis=0), low[:blk], high[:blk]


def halves_out(odd, wgrad, keep, send, at):
    shards, slot, _ = keep.shape
    rows = wgrad.shape[0] // shards // 2
    bit = odd.astype(jnp.int32)
    for s in range(shards):
        mine = pl.ds((s * 2 + bit) * rows, rows)
        other = pl.ds((s * 2 + 1 - bit) * rows, rows)
        keep[s, :rows, :] = wgrad[mine, :]
        start = at + s * slot
        send[start : start + rows, :] = wgrad[other, :].astype(BF16)


def first_kernel(
    count_ref, features, core_in, cross_in, singles, part, weights,
    entries, far, halo, hidden, slope, core_out, cross_out, picked,
):
    blk = features.shape[0] // 2
    per = singles.shape[0] // 2
    count = count_ref[:1, :]
    odd, _, _ = place()
    from_next, from_prev = halo_sides(odd, core_in[...].astype(F32), cross_in[...].astype(F32))
    table = stacked([from_next[blk : blk + per], from_prev[blk : blk + per]], blk, -1.0)
    entries[...] = table
    columns = table.T
    for at in range(2 * per):
        far[at] = by_targets(columns, at, blk)
    after, before = from_next[:blk].astype(BF16), from_prev[:blk].astype(BF16)
    halo[0] = after
    halo[1] = before
    front, back = features[:blk, :], features[blk:, :]
    sources = [
        jnp.concatenate([after, back], axis=0),
        jnp.concatenate([before, front], axis=0),
    ]
    pre = part[...] + outer_part(far, singles, sources, weights, picked)
    mask = row_mask(2 * blk, blk, count)
    value, grad = sigmoid_terms(pre)
    field = (value * mask).astype(BF16)
    hidden[...] = field
    slope[...] = grad * mask
    head = field[:blk]
    tail = jnp.where(count == 2, field[blk:], head)
    core_out[...], cross_out[...] = exchange_sides(odd, tail, head)


def middle_kernel(hidden, pairs, entries, weights, part, far_turned, picked):
    part[...] = middle_part(pairs, hidden[...], weights, picked)
    for at in range(far_turned.shape[0]):
        far_turned[at] = by_sources(entries, at, entries.shape[1])


def second_kernel(
    count_ref, features, hidden, core_in, cross_in, far, singles, part, weights, cotangent,
    far_turned, pairs_turned, singles_turned,
    result, grads_out, own_out, keep, core_out, cross_out, picked, pulled, wgrad,
):
    blk = features.shape[0] // 2
    count = count_ref[:1, :]
    both = count == 2
    odd, _, _ = place()
    after, before = halo_sides(odd, core_in[...], cross_in[...])
    front, back = hidden[:blk, :], hidden[blk:, :]
    low = jnp.concatenate([after, back], axis=0)
    high = jnp.concatenate([before, front], axis=0)
    total = part[...] + outer_part(far, singles, [low, high], weights, picked)
    total = total + features[...].astype(F32)
    mask = row_mask(2 * blk, blk, count)
    value, grad = sigmoid_terms(total)
    result[...] = (value * mask).astype(BF16)
    grads = (cotangent[...].astype(F32) * grad * mask).astype(BF16)
    grads_out[...] = grads
    sources = [low, hidden[...], high]
    sums = []
    for kind in range(KINDS):
        pull(far_turned, pairs_turned, singles_turned, grads, pulled, kind)
        sums.append(source_sums(pulled, weights, kind))
        weight_sums(pulled, sources[kind], wgrad, kind)
    own, to_next, to_prev = split_sums(sums, both, blk)
    own_out[...] = own
    core, cross = exchange_sides(odd, to_next, to_prev)
    core_out[:blk, :] = core.astype(BF16)
    cross_out[...] = cross.astype(BF16)
    halves_out(odd, wgrad, keep, core_out, blk)


def joined(own, odd, both, core_in, cross_in, blk):
    from_next, from_prev = halo_sides(odd, core_in, cross_in)
    first = own[:blk] + from_prev + jnp.where(both, 0.0, from_next)
    second = own[blk:] + jnp.where(both, from_next, 0.0)
    return jnp.concatenate([first, second], axis=0)


def third_kernel(
    count_ref, features, halo, own, core_in, cross_in, slope,
    far_turned, pairs_turned, singles_turned,
    pulled, keep, core_out, wgrad,
):
    blk = features.shape[0] // 2
    both = count_ref[:1, :] == 2
    odd, _, _ = place()
    core, cross = core_in[:blk, :].astype(F32), cross_in[...].astype(F32)
    summed = joined(own[...], odd, both, core, cross, blk)
    grads = (summed * slope[...]).astype(BF16)
    sources = [
        jnp.concatenate([halo[0], features[blk:, :]], axis=0),
        features[...],
        jnp.concatenate([halo[1], features[:blk, :]], axis=0),
    ]
    for kind in range(KINDS):
        pull(far_turned, pairs_turned, singles_turned, grads, pulled, kind)
    for kind in range(KINDS):
        weight_sums(pulled, sources[kind], wgrad, kind)
    halves_out(odd, wgrad, keep, core_out, 0)


def fourth_kernel(count_ref, pulled, weights, grads_in, own_out, core_out, cross_out):
    blk = grads_in.shape[0] // 2
    both = count_ref[:1, :] == 2
    odd, _, _ = place()
    sums = [source_sums(pulled, weights, kind) for kind in range(KINDS)]
    own, to_next, to_prev = split_sums(sums, both, blk)
    own_out[...] = own + grads_in[...].astype(F32)
    core, cross = exchange_sides(odd, to_next, to_prev)
    core_out[...] = core.astype(BF16)
    cross_out[...] = cross.astype(BF16)


def last_kernel(count_ref, own, core_in, cross_in, input_grad):
    blk = own.shape[0] // 2
    both = count_ref[:1, :] == 2
    odd, _, _ = place()
    core, cross = core_in[...].astype(F32), cross_in[...].astype(F32)
    input_grad[...] = joined(own[...], odd, both, core, cross, blk).astype(BF16)


def shards_kernel(keep, core, own, *sends):
    shards, slot, _ = keep.shape
    blk = core.shape[0] - shards * slot
    me = lax.axis_index("grp")
    for d in range(shards):
        to = me ^ d
        at = pl.ds(pl.multiple_of(blk + to * slot, 16), slot)
        value = keep[to] + core[at, :].astype(F32)
        if d == 0:
            own[...] = value
        else:
            sends[d - 1][...] = value.astype(BF16)


def after(first, later):
    return lax.optimization_barrier((first, later))[1]


def either_order(second, mine, other):
    parts = [jnp.where(second, other, mine), jnp.where(second, mine, other)]
    return jnp.concatenate(parts, axis=0)


def added(value, others):
    value = value.astype(F32)
    for other in others:
        value = value + other.astype(F32)
    return value


def call(kernel, outs, *args, scratch=(), micros=1, far=False):
    vmem = pl.BlockSpec(memory_space=pltpu.VMEM)
    return pl.pallas_call(
        kernel,
        out_shape=[jax.ShapeDtypeStruct(shape, kind) for shape, kind in outs],
        in_specs=[pl.BlockSpec(memory_space=pltpu.HBM if far else pltpu.VMEM)] * len(args),
        out_specs=[vmem] * len(outs),
        scratch_shapes=[pltpu.VMEM(*one) if isinstance(one, tuple) else one for one in scratch],
        compiler_params=pltpu.CompilerParams(vmem_limit_bytes=LIMIT),
        cost_estimate=pl.CostEstimate(
            flops=micros * 10**9, bytes_accessed=micros * 3 * 10**6, transcendentals=0
        ),
    )(*args)


def on_device(
    features, source_rows, target_codes, block_count, weight_one, weight_two, out_cotangent
):
    offsets, _, blk = source_rows.shape
    rows, channels = features.shape
    n_grp, n_tile = lax.axis_size("grp"), lax.axis_size("tile")
    per = offsets // KINDS
    flat_one = weight_one.reshape(offsets * channels, channels)
    flat_two = weight_two.reshape(offsets * channels, channels)
    packed = blk + per + (-per % 16)
    half = offsets * channels // n_grp // 2
    slot = half + (-half % 16)
    field, block = ((rows, channels), BF16), ((blk, channels), BF16)
    summed = ((rows, channels), F32)
    keep_shape = ((n_grp, slot, channels), F32)
    core_shape = ((blk + n_grp * slot, channels), BF16)
    pairs_shape = ((per, 2 * blk, 2 * blk), BF16)
    single_shape, turned_shape = ((2 * per, 2 * blk, blk), BF16), ((2 * per, blk, 2 * blk), BF16)
    inner, outer = ((rows, per * channels), BF16), ((rows, 2 * per * channels), BF16)
    pulled = ((rows, offsets * channels), BF16)
    wgrad = ((offsets * channels, channels), F32)

    near, core, cross, count = call(
        pack_kernel,
        [
            ((4 * per + (-4 * per % 8), blk), F32), ((packed, channels), BF16),
            ((packed, channels), BF16), ((8, channels), jnp.int32),
        ],
        *[
            pltpu.with_memory_space_constraint(value, pltpu.HBM)
            for value in (features, source_rows, target_codes.T)
        ],
        scratch=[
            pltpu.VMEM(features.shape, BF16), pltpu.VMEM(source_rows.shape, jnp.int32),
            pltpu.VMEM(target_codes.shape[::-1], jnp.int32),
            pltpu.SemaphoreType.DMA((3,)),
        ],
        micros=3,
        far=True,
    )
    cross, core = crossed(cross), swapped(core, "tile", 1)
    pairs, singles, pairs_turned, singles_turned, part = call(
        local_kernel,
        [pairs_shape, single_shape, pairs_shape, turned_shape, summed],
        near, features, flat_one,
        scratch=[inner],
        micros=2,
    )
    entries, far, halo, hidden, slope, core, cross = call(
        first_kernel,
        [
            ((2 * per + (-2 * per % 8), blk), F32), single_shape, ((2, blk, channels), BF16),
            field, summed, block, block,
        ],
        count, features, core, cross, singles, part, flat_one,
        scratch=[outer],
        micros=2,
    )
    cross, core = crossed(cross), swapped(core, "tile", 1)
    part, far_turned = call(
        middle_kernel,
        [summed, turned_shape],
        hidden, pairs, entries, flat_two,
        scratch=[inner],
        micros=1,
    )
    result, grad_sum, own, keep_two, core_two, cross = call(
        second_kernel,
        [field, field, summed, keep_shape, core_shape, block],
        count, features, hidden, core, cross, far, singles, part, flat_two, out_cotangent,
        far_turned, pairs_turned, singles_turned,
        scratch=[outer, pulled, wgrad],
        micros=4,
    )
    cross, core_two = crossed(cross), swapped(core_two, "tile", 1)
    shard = (slot, channels)
    shards = [(shard, F32)] + [(shard, BF16)] * (n_grp - 1)
    mine_two, *sends_two = call(shards_kernel, shards, keep_two, core_two)
    got_two = [swapped(send, "grp", d + 1) for d, send in enumerate(sends_two)]
    own = after(sends_two[-1], own)
    held, keep_one, core_one = call(
        third_kernel,
        [pulled, keep_shape, ((n_grp * slot, channels), BF16)],
        count, features, halo, own, core_two, cross, slope,
        far_turned, pairs_turned, singles_turned,
        scratch=[wgrad],
        micros=2,
    )
    core_one = swapped(core_one, "tile", 1)
    mine_one, *sends_one = call(shards_kernel, shards, keep_one, core_one)
    got_one = [swapped(send, "grp", d + 1) for d, send in enumerate(sends_one)]
    own, core, cross = call(
        fourth_kernel,
        [summed, block, block],
        count, after(sends_one[-1], held), flat_one, grad_sum,
    )
    two = added(mine_two, got_two).astype(BF16)
    steps = [1 << b for b in range(1, (n_tile - 1).bit_length())]
    other_two = swapped(two, "tile", steps[-1])
    one = added(mine_one, got_one).astype(BF16)
    for at, bits in enumerate(steps):
        other_one = swapped(one, "tile", bits)
        two = added(two, [other_two])
        if at + 1 < len(steps):
            two = two.astype(BF16)
            two = after(one, two)
            other_two = swapped(two, "tile", steps[-2 - at])
            one = added(one, [other_one]).astype(BF16)
            if at == 0:
                one, core, cross = lax.optimization_barrier((one, core, cross))
    cross, core = crossed(cross), swapped(core, "tile", 1)
    (input_grad,) = call(last_kernel, [field], count, own, core, cross)
    scale = float(n_grp * n_tile * rows) ** (-0.5)
    odd = lax.axis_index("tile") % 2 == 1

    def finished(part):
        part = part[:half]
        other = swapped(part, "tile", 1)
        return either_order(odd, part.astype(F32) * scale, other.astype(F32) * scale)

    other_one = after(cross, other_one)
    two = finished(two.astype(BF16))
    one = finished(added(one, [other_one]).astype(BF16))
    return (result, input_grad, one, two)


def solution(mesh):
    in_specs = (
        P(("grp", "tile"), None),
        P(None, ("grp", "tile"), None),
        P(None, ("grp", "tile")),
        P(("grp", "tile")),
        P(),
        P(),
        P(("grp", "tile"), None),
    )
    out_specs = (P(("grp", "tile"), None), P(("grp", "tile"), None), P("grp", None), P("grp", None))
    return jax.shard_map(
        on_device, mesh=mesh, in_specs=in_specs, out_specs=out_specs, check_vma=False
    )
```

```python
import functools

import jax
import jax.numpy as jnp
from jax import lax
from jax.experimental import pallas as pl
from jax.experimental.pallas import tpu as pltpu
from jax.sharding import PartitionSpec as P

F32 = jnp.float32
BF16 = jnp.bfloat16
KINDS = 3
LIMIT = 28 * 1024 * 1024
NT = (((1,), (1,)), ((), ()))


def swapped(value, axis, bits):
    count = lax.axis_size(axis)
    return lax.ppermute(value, axis, [(i, i ^ bits) for i in range(count) if i ^ bits < count])


def crossed(value):
    groups, count = lax.axis_size("grp"), lax.axis_size("tile")
    pairs = []
    for i in range(groups * count):
        group, tile = divmod(i, count)
        other = ((tile + 1) ^ 1) - 1
        if 0 <= other < count:
            pairs.append((i, group * count + other))
        elif (group ^ 1) < groups:
            pairs.append((i, (group ^ 1) * count + tile))
    return lax.ppermute(value, ("grp", "tile"), pairs)


def sigmoid_terms(values):
    sigma = jax.nn.sigmoid(values)
    return values * sigma, sigma * (1.0 + values * (1.0 - sigma))


def place():
    tile = lax.axis_index("tile")
    return tile % 2 == 1, tile > 0, tile < lax.axis_size("tile") - 1


def halo_sides(odd, core, cross):
    return jnp.where(odd, cross, core), jnp.where(odd, core, cross)


def exchange_sides(odd, to_next, to_prev):
    return jnp.where(odd, to_prev, to_next), jnp.where(odd, to_next, to_prev)


def row_mask(rows, blk, count):
    block = lax.broadcasted_iota(jnp.int32, (rows, count.shape[1]), 0) // blk
    return (block < count).astype(F32)


def of_kind(values, kind):
    return [values[i : i + 1] for i in range(kind, values.shape[0], KINDS)]


def stacked(rows, blk, fill):
    spare = -len(rows) % 8
    if spare:
        rows = rows + [jnp.full((spare, blk), fill, F32)]
    return jnp.concatenate(rows, axis=0)


def pack_kernel(
    features_in, rows_in, codes_in, near, core_out, cross_out, count_out,
    features, source_rows, codes, done,
):
    copies = []
    for at, (source, target) in enumerate(
        [(rows_in, source_rows), (codes_in, codes), (features_in, features)]
    ):
        copies.append(pltpu.make_async_copy(source, target, done.at[at]))
        copies[-1].start()
    for copy in copies:
        copy.wait()
    offsets, _, blk = source_rows.shape
    per = offsets // KINDS
    count = jnp.where(codes[:1, KINDS - 1 : KINDS] // 2 == 2, 1, 2)
    count = jnp.broadcast_to(count, (1, blk))
    count_out[...] = jnp.broadcast_to(count, count_out.shape)
    both = count == 2
    odd, has_prev, has_next = place()
    diagonal = lax.broadcasted_iota(jnp.int32, (offsets, offsets), 0) == lax.broadcasted_iota(
        jnp.int32, (offsets, offsets), 1
    )
    coded = []
    for j in range(2):
        rows = source_rows[:, j, :]
        block = lax.rem(codes[j : j + 1, :], 2).astype(F32)
        block = jnp.sum(jnp.where(diagonal, block, 0.0), axis=1, keepdims=True)
        live = (rows >= 0) & (count > j)
        coded.append(jnp.where(live, rows.astype(F32) + blk * block, -1.0))
    first, second = coded
    inner = jnp.where(both, first, -1.0)
    rows = of_kind(second, 0) + of_kind(first, 1) + of_kind(second, 1) + of_kind(inner, 2)
    near[...] = stacked(rows, blk, -1.0)
    to_prev = of_kind(jnp.where(has_prev, first, -1.0), 0)
    last = jnp.where(both, second, first)
    to_next = of_kind(jnp.where(has_next, last, -1.0), 2)
    pad = core_out.shape[0] - blk - per
    fill = [jnp.full((pad, blk), -1.0, F32)]
    to_prev = jnp.concatenate(to_prev + fill, axis=0).astype(BF16)
    to_next = jnp.concatenate(to_next + fill, axis=0).astype(BF16)
    front, back = features[:blk, :], features[blk:, :]
    tail = jnp.where(both, back, front)
    core_out[:blk, :], cross_out[:blk, :] = exchange_sides(odd, tail, front)
    core_out[blk:, :], cross_out[blk:, :] = exchange_sides(odd, to_next, to_prev)


def by_targets(columns, at, blk):
    lane = lax.broadcasted_iota(jnp.int32, (blk, blk), 1).astype(F32).astype(BF16)
    one, zero = jnp.ones((blk, blk), BF16), jnp.zeros((blk, blk), BF16)
    entry = jnp.broadcast_to(columns[:, at : at + 1], (blk, blk)).astype(BF16)
    halves = [jnp.where(entry == lane + b * blk, one, zero) for b in range(2)]
    return jnp.concatenate(halves, axis=0)


def by_sources(entries, at, blk):
    sub = lax.broadcasted_iota(jnp.int32, (blk, blk), 0).astype(F32).astype(BF16)
    one, zero = jnp.ones((blk, blk), BF16), jnp.zeros((blk, blk), BF16)
    entry = jnp.broadcast_to(entries[at : at + 1, :], (blk, blk)).astype(BF16)
    halves = [jnp.where(entry == sub + b * blk, one, zero) for b in range(2)]
    return jnp.concatenate(halves, axis=1)


def weights_of(weights, kind, per, axis):
    channels = weights.shape[1]
    parts = []
    for i in range(per):
        at = (i * KINDS + kind) * channels
        parts.append(weights[at : at + channels, :])
    return jnp.concatenate(parts, axis=axis)


def middle_part(pairs, source, weights, picked):
    per, channels = pairs.shape[0], weights.shape[1]
    for i in range(per):
        got = jnp.dot(pairs[i], source, preferred_element_type=F32)
        picked[:, i * channels : (i + 1) * channels] = got.astype(BF16)
    wide = weights_of(weights, 1, per, 0)
    return jnp.dot(picked[...], wide, preferred_element_type=F32)


def outer_part(far, singles, sources, weights, picked):
    per, channels = singles.shape[0] // 2, weights.shape[1]
    for side, source in enumerate(sources):
        for i in range(per):
            at = side * per + i
            select = jnp.concatenate([far[at], singles[at]], axis=1)
            got = jnp.dot(select, source, preferred_element_type=F32)
            picked[:, at * channels : (at + 1) * channels] = got.astype(BF16)
    wide = jnp.concatenate([weights_of(weights, kind, per, 0) for kind in (0, 2)], axis=0)
    return jnp.dot(picked[...], wide, preferred_element_type=F32)


def local_kernel(
    near, features, weights, pairs, singles, pairs_turned, singles_turned, part, picked
):
    blk = near.shape[1]
    per = pairs.shape[0]
    columns = near[...].T
    for i in range(per):
        at, to = per + i, 2 * per + i
        pairs[i, :, :blk] = by_targets(columns, at, blk)
        pairs[i, :, blk:] = by_targets(columns, to, blk)
        pairs_turned[i, :blk, :] = by_sources(near, at, blk)
        pairs_turned[i, blk:, :] = by_sources(near, to, blk)
    part[...] = middle_part(pairs, features[...], weights, picked)
    for i in range(per):
        for side, at in ((0, i), (1, 3 * per + i)):
            singles[side * per + i] = by_targets(columns, at, blk)
            singles_turned[side * per + i] = by_sources(near, at, blk)


def pull_middle(pairs_turned, grads, pulled, base):
    per, channels = pairs_turned.shape[0], grads.shape[1]
    for i in range(per):
        got = jnp.dot(pairs_turned[i], grads, preferred_element_type=F32)
        at = base + i * channels
        pulled[:, at : at + channels] = got.astype(BF16)


def pull_outer(far_turned, singles_turned, grads, pulled, side, base=0):
    per, channels = far_turned.shape[0] // 2, grads.shape[1]
    for i in range(side * per, (side + 1) * per):
        select = jnp.concatenate([far_turned[i], singles_turned[i]], axis=0)
        got = jnp.dot(select, grads, preferred_element_type=F32)
        at = base + i * channels
        pulled[:, at : at + channels] = got.astype(BF16)


def side_of(pulled, side, sides):
    wide = pulled.shape[1] // sides
    return pulled[:, side * wide : (side + 1) * wide]


def source_sums(held, weights, kind):
    per = weights.shape[0] // weights.shape[1] // KINDS
    wide = weights_of(weights, kind, per, 1)
    return lax.dot_general(held, wide, NT, preferred_element_type=F32)


def weight_sums(held, source, wgrad, kind):
    channels = wgrad.shape[1]
    terms = jnp.dot(source.T, held, preferred_element_type=F32)
    for i in range(terms.shape[1] // channels):
        at = (i * KINDS + kind) * channels
        wgrad[at : at + channels, :] = terms[:, i * channels : (i + 1) * channels]


def split_sums(sums, both, blk):
    low, mid, high = sums
    first = mid[:blk] + jnp.where(both, high[blk:], 0.0)
    second = mid[blk:] + low[blk:]
    return jnp.concatenate([first, second], axis=0), low[:blk], high[:blk]


def halves_out(odd, wgrad, keep, send, at):
    shards, slot, _ = keep.shape
    rows = wgrad.shape[0] // shards // 2
    bit = odd.astype(jnp.int32)
    for s in range(shards):
        mine = pl.ds((s * 2 + bit) * rows, rows)
        other = pl.ds((s * 2 + 1 - bit) * rows, rows)
        keep[s, :rows, :] = wgrad[mine, :]
        start = at + s * slot
        send[start : start + rows, :] = wgrad[other, :].astype(BF16)


def first_kernel(
    count_ref, features, core_in, cross_in, singles, part, weights,
    entries, far, halo, hidden, slope, core_out, cross_out, picked,
):
    blk = features.shape[0] // 2
    per = singles.shape[0] // 2
    count = count_ref[:1, :]
    odd, _, _ = place()
    from_next, from_prev = halo_sides(odd, core_in[...].astype(F32), cross_in[...].astype(F32))
    table = stacked([from_next[blk : blk + per], from_prev[blk : blk + per]], blk, -1.0)
    entries[...] = table
    columns = table.T
    for at in range(2 * per):
        far[at] = by_targets(columns, at, blk)
    after, before = from_next[:blk].astype(BF16), from_prev[:blk].astype(BF16)
    halo[0] = after
    halo[1] = before
    front, back = features[:blk, :], features[blk:, :]
    sources = [
        jnp.concatenate([after, back], axis=0),
        jnp.concatenate([before, front], axis=0),
    ]
    pre = part[...] + outer_part(far, singles, sources, weights, picked)
    mask = row_mask(2 * blk, blk, count)
    value, grad = sigmoid_terms(pre)
    field = (value * mask).astype(BF16)
    hidden[...] = field
    slope[...] = grad * mask
    head = field[:blk]
    tail = jnp.where(count == 2, field[blk:], head)
    core_out[...], cross_out[...] = exchange_sides(odd, tail, head)


def middle_kernel(hidden, pairs, entries, weights, part, far_turned, picked):
    part[...] = middle_part(pairs, hidden[...], weights, picked)
    for at in range(far_turned.shape[0]):
        far_turned[at] = by_sources(entries, at, entries.shape[1])


def outer_sources(hidden, odd, core_in, cross_in, blk):
    after, before = halo_sides(odd, core_in[...], cross_in[...])
    low = jnp.concatenate([after, hidden[blk:, :]], axis=0)
    return low, jnp.concatenate([before, hidden[:blk, :]], axis=0)


def second_kernel(
    count_ref, features, hidden, core_in, cross_in, far, singles, part, weights, cotangent,
    far_turned, singles_turned,
    result, grads_out, own_out, pulled, core_out, cross_out, picked,
):
    blk = features.shape[0] // 2
    count = count_ref[:1, :]
    both = count == 2
    odd, _, _ = place()
    low, high = outer_sources(hidden, odd, core_in, cross_in, blk)
    total = part[...] + outer_part(far, singles, [low, high], weights, picked)
    total = total + features[...].astype(F32)
    mask = row_mask(2 * blk, blk, count)
    value, grad = sigmoid_terms(total)
    result[...] = (value * mask).astype(BF16)
    grads = (cotangent[...].astype(F32) * grad * mask).astype(BF16)
    grads_out[...] = grads
    sums = []
    for side, kind in enumerate((0, 2)):
        pull_outer(far_turned, singles_turned, grads, pulled, side)
        sums.append(source_sums(side_of(pulled, side, 2), weights, kind))
    low, high = sums
    own_out[:blk, :] = jnp.where(both, high[blk:], 0.0)
    own_out[blk:, :] = low[blk:]
    core, cross = exchange_sides(odd, low[:blk], high[:blk])
    core_out[...] = core.astype(BF16)
    cross_out[...] = cross.astype(BF16)


def second_rest_kernel(
    hidden, core_in, cross_in, weights, grads, pulled, own_in, pairs_turned,
    own_out, keep, core_out, middle, wgrad,
):
    blk = hidden.shape[0] // 2
    odd, _, _ = place()
    pull_middle(pairs_turned, grads[...], middle, 0)
    own_out[...] = own_in[...] + source_sums(middle[...], weights, 1)
    low, high = outer_sources(hidden, odd, core_in, cross_in, blk)
    weight_sums(middle[...], hidden[...], wgrad, 1)
    weight_sums(side_of(pulled, 0, 2), low, wgrad, 0)
    weight_sums(side_of(pulled, 1, 2), high, wgrad, 2)
    halves_out(odd, wgrad, keep, core_out, 0)


def joined(own, odd, both, core_in, cross_in, blk):
    from_next, from_prev = halo_sides(odd, core_in, cross_in)
    first = own[:blk] + from_prev + jnp.where(both, 0.0, from_next)
    second = own[blk:] + jnp.where(both, from_next, 0.0)
    return jnp.concatenate([first, second], axis=0)


def third_kernel(
    count_ref, features, halo, own, core_in, cross_in, slope,
    far_turned, pairs_turned, singles_turned,
    pulled, keep, core_out, wgrad,
):
    blk = features.shape[0] // 2
    both = count_ref[:1, :] == 2
    odd, _, _ = place()
    core, cross = core_in[...].astype(F32), cross_in[...].astype(F32)
    summed = joined(own[...], odd, both, core, cross, blk)
    grads = (summed * slope[...]).astype(BF16)
    sources = [
        jnp.concatenate([halo[0], features[blk:, :]], axis=0),
        features[...],
        jnp.concatenate([halo[1], features[:blk, :]], axis=0),
    ]
    for side in range(2):
        pull_outer(far_turned, singles_turned, grads, pulled, side)
    pull_middle(pairs_turned, grads, pulled, pulled.shape[1] // KINDS * 2)
    for at, kind in enumerate((0, 2, 1)):
        weight_sums(side_of(pulled, at, KINDS), sources[kind], wgrad, kind)
    halves_out(odd, wgrad, keep, core_out, 0)


def fourth_kernel(count_ref, pulled, weights, grads_in, own_out, core_out, cross_out):
    blk = grads_in.shape[0] // 2
    both = count_ref[:1, :] == 2
    odd, _, _ = place()
    low, high, middle = [
        source_sums(side_of(pulled, at, KINDS), weights, kind)
        for at, kind in enumerate((0, 2, 1))
    ]
    own, to_next, to_prev = split_sums([low, middle, high], both, blk)
    own_out[...] = own + grads_in[...].astype(F32)
    core, cross = exchange_sides(odd, to_next, to_prev)
    core_out[...] = core.astype(BF16)
    cross_out[...] = cross.astype(BF16)


def both_halves(odd, mine, other, scale, out):
    half = out.shape[0] // 2
    mine, other = mine[:half, :].astype(F32) * scale, other[:half, :].astype(F32) * scale
    out[:half, :] = jnp.where(odd, other, mine)
    out[half:, :] = jnp.where(odd, mine, other)


def last_kernel(
    scale, count_ref, own, core_in, cross_in, mine, near, far_off, both_off, input_grad, out
):
    blk = own.shape[0] // 2
    both = count_ref[:1, :] == 2
    odd, _, _ = place()
    core, cross = core_in[...].astype(F32), cross_in[...].astype(F32)
    input_grad[...] = joined(own[...], odd, both, core, cross, blk).astype(BF16)
    upper = (lax.axis_index("tile") // 2) % 2 == 1
    half, part = out.shape[0] // 2, mine.shape[0]
    slot = half + (-half % 16)
    values = [ref[...].astype(F32) * scale for ref in (mine, far_off, near, both_off)]
    low = [jnp.where(upper, values[1], values[0]), jnp.where(upper, values[3], values[2])]
    high = [jnp.where(upper, values[0], values[1]), jnp.where(upper, values[2], values[3])]
    for side in range(2):
        at = side * half
        out[at : at + part, :] = jnp.where(odd, low[1 - side], low[side])
        rest = jnp.where(odd, high[1 - side], high[side])
        skip = 2 * part - slot
        out[at + part : at + half, :] = rest[skip : skip + half - part]


def rows_kernel(scale, mine, other, out):
    odd, _, _ = place()
    both_halves(odd, mine, other, scale, out)


def quarters_kernel(keep, core, kept, send):
    shards, slot, _ = keep.shape
    part = kept.shape[1]
    upper = (lax.axis_index("tile") // 2) % 2 == 1
    for s in range(shards):
        value = keep[s] + core[s * slot : (s + 1) * slot, :].astype(F32)
        low, high = value[:part], value[slot - part :]
        kept[s] = jnp.where(upper, high, low)
        send[s * part : (s + 1) * part, :] = jnp.where(upper, low, high).astype(BF16)


def shards_kernel(keep, core, own, *sends):
    shards, slot, _ = keep.shape
    blk = core.shape[0] - shards * slot
    me = lax.axis_index("grp")
    for d in range(shards):
        to = me ^ d
        at = pl.ds(pl.multiple_of(blk + to * slot, 16), slot)
        value = keep[to] + core[at, :].astype(F32)
        if d == 0:
            own[...] = value
        else:
            sends[d - 1][...] = value.astype(BF16)


def after(first, later):
    return lax.optimization_barrier((first, later))[1]


def added(value, others):
    value = value.astype(F32)
    for other in others:
        value = value + other.astype(F32)
    return value


def call(kernel, outs, *args, scratch=(), micros=1, far=False):
    vmem = pl.BlockSpec(memory_space=pltpu.VMEM)
    return pl.pallas_call(
        kernel,
        out_shape=[jax.ShapeDtypeStruct(shape, kind) for shape, kind in outs],
        in_specs=[pl.BlockSpec(memory_space=pltpu.HBM if far else pltpu.VMEM)] * len(args),
        out_specs=[vmem] * len(outs),
        scratch_shapes=[pltpu.VMEM(*one) if isinstance(one, tuple) else one for one in scratch],
        compiler_params=pltpu.CompilerParams(vmem_limit_bytes=LIMIT),
        cost_estimate=pl.CostEstimate(
            flops=micros * 10**9, bytes_accessed=micros * 3 * 10**6, transcendentals=0
        ),
    )(*args)


def on_device(
    features, source_rows, target_codes, block_count, weight_one, weight_two, out_cotangent
):
    offsets, _, blk = source_rows.shape
    rows, channels = features.shape
    n_grp, n_tile = lax.axis_size("grp"), lax.axis_size("tile")
    per = offsets // KINDS
    flat_one = weight_one.reshape(offsets * channels, channels)
    flat_two = weight_two.reshape(offsets * channels, channels)
    packed = blk + per + (-per % 16)
    half = offsets * channels // n_grp // 2
    slot = half + (-half % 16)
    field, block = ((rows, channels), BF16), ((blk, channels), BF16)
    summed = ((rows, channels), F32)
    keep_shape = ((n_grp, slot, channels), F32)
    core_shape = ((blk + n_grp * slot, channels), BF16)
    pairs_shape = ((per, 2 * blk, 2 * blk), BF16)
    single_shape, turned_shape = ((2 * per, 2 * blk, blk), BF16), ((2 * per, blk, 2 * blk), BF16)
    inner, outer = ((rows, per * channels), BF16), ((rows, 2 * per * channels), BF16)
    pulled = ((rows, offsets * channels), BF16)
    wgrad = ((offsets * channels, channels), F32)

    near, core, cross, count = call(
        pack_kernel,
        [
            ((4 * per + (-4 * per % 8), blk), F32), ((packed, channels), BF16),
            ((packed, channels), BF16), ((8, channels), jnp.int32),
        ],
        *[
            pltpu.with_memory_space_constraint(value, pltpu.HBM)
            for value in (features, source_rows, target_codes.T)
        ],
        scratch=[
            pltpu.VMEM(features.shape, BF16), pltpu.VMEM(source_rows.shape, jnp.int32),
            pltpu.VMEM(target_codes.shape[::-1], jnp.int32),
            pltpu.SemaphoreType.DMA((3,)),
        ],
        micros=3,
        far=True,
    )
    cross, core = crossed(cross), swapped(core, "tile", 1)
    pairs, singles, pairs_turned, singles_turned, part = call(
        local_kernel,
        [pairs_shape, single_shape, pairs_shape, turned_shape, summed],
        near, features, flat_one,
        scratch=[inner],
        micros=2,
    )
    entries, far, halo, hidden, slope, core, cross = call(
        first_kernel,
        [
            ((2 * per + (-2 * per % 8), blk), F32), single_shape, ((2, blk, channels), BF16),
            field, summed, block, block,
        ],
        count, features, core, cross, singles, part, flat_one,
        scratch=[outer],
        micros=2,
    )
    cross, core = crossed(cross), swapped(core, "tile", 1)
    part, far_turned = call(
        middle_kernel,
        [summed, turned_shape],
        hidden, pairs, entries, flat_two,
        scratch=[inner],
        micros=1,
    )
    result, grad_sum, own, held, core_sum, cross_sum = call(
        second_kernel,
        [field, field, summed, outer, block, block],
        count, features, hidden, core, cross, far, singles, part, flat_two, out_cotangent,
        far_turned, singles_turned,
        scratch=[outer],
        micros=3,
    )
    cross_sum, core_sum = crossed(cross_sum), swapped(core_sum, "tile", 1)
    own, keep_two, core_two = call(
        second_rest_kernel,
        [summed, keep_shape, ((n_grp * slot, channels), BF16)],
        hidden, core, cross, flat_two, grad_sum, held, own, pairs_turned,
        scratch=[inner, wgrad],
        micros=1,
    )
    core_two = swapped(core_two, "tile", 1)
    shard = (slot, channels)
    shards = [(shard, F32)] + [(shard, BF16)] * (n_grp - 1)
    part = slot // 2 + (-(slot // 2) % 16)
    quarter = (part, channels)
    steps = [1 << b for b in range(1, (n_tile - 1).bit_length())]
    kept_two, send_two = call(
        quarters_kernel,
        [((n_grp, part, channels), F32), ((n_grp * part, channels), BF16)],
        keep_two, core_two,
    )
    held, keep_one, core_one = call(
        third_kernel,
        [pulled, keep_shape, ((n_grp * slot, channels), BF16)],
        count, features, halo, own, core_sum, cross_sum, slope,
        far_turned, pairs_turned, singles_turned,
        scratch=[wgrad],
        micros=2,
    )
    core_one = swapped(core_one, "tile", 1)
    near_two = swapped(send_two, "tile", steps[0])
    mine_one, *sends_one = call(shards_kernel, shards, keep_one, core_one)
    got_one = [swapped(send, "grp", d + 1) for d, send in enumerate(sends_one)]
    own, core, cross = call(
        fourth_kernel,
        [summed, block, block],
        count, after(sends_one[-1], held), flat_one, grad_sum,
    )
    mine_two, *sends_two = call(
        shards_kernel,
        [(quarter, F32)] + [(quarter, BF16)] * (n_grp - 1),
        after(sends_one[-1], kept_two), near_two,
    )
    got_two = [swapped(send, "grp", d + 1) for d, send in enumerate(sends_two)]
    one = added(mine_one, got_one).astype(BF16)
    two = added(mine_two, got_two)
    for at, bits in enumerate(steps):
        other_one = swapped(one, "tile", bits)
        if at + 1 < len(steps):
            two = two.astype(BF16)
            two = after(one, two)
            other_two = swapped(two, "tile", steps[at + 1])
            two = added(two, [other_two])
            one = added(one, [other_one]).astype(BF16)
    two = two.astype(BF16)
    core, cross = lax.optimization_barrier((one, core, cross))[1:]
    cross, core = crossed(cross), swapped(core, "tile", 1)
    near, far_off, both_off = [swapped(two, "tile", bits) for bits in (1, steps[0], steps[0] + 1)]
    scale = float(n_grp * n_tile * rows) ** (-0.5)
    shard_out = ((2 * half, channels), F32)
    input_grad, two = call(
        functools.partial(last_kernel, scale),
        [field, shard_out],
        count, own, core, cross, two, near, far_off, both_off,
    )
    one = added(one, [other_one]).astype(BF16)
    (one,) = call(
        functools.partial(rows_kernel, scale), [shard_out], one, swapped(one, "tile", 1)
    )
    return (result, input_grad, one, two)


def solution(mesh):
    in_specs = (
        P(("grp", "tile"), None),
        P(None, ("grp", "tile"), None),
        P(None, ("grp", "tile")),
        P(("grp", "tile")),
        P(),
        P(),
        P(("grp", "tile"), None),
    )
    out_specs = (P(("grp", "tile"), None), P(("grp", "tile"), None), P("grp", None), P("grp", None))
    return jax.shard_map(
        on_device, mesh=mesh, in_specs=in_specs, out_specs=out_specs, check_vma=False
    )
```

```python
import functools

import jax
import jax.numpy as jnp
from jax import lax
from jax.experimental import pallas as pl
from jax.experimental.pallas import tpu as pltpu
from jax.sharding import PartitionSpec as P

F32 = jnp.float32
BF16 = jnp.bfloat16
KINDS = 3
LIMIT = 28 * 1024 * 1024
NT = (((1,), (1,)), ((), ()))


def swapped(value, axis, bits):
    count = lax.axis_size(axis)
    return lax.ppermute(value, axis, [(i, i ^ bits) for i in range(count) if i ^ bits < count])


def crossed(value):
    groups, count = lax.axis_size("grp"), lax.axis_size("tile")
    pairs = []
    for i in range(groups * count):
        group, tile = divmod(i, count)
        other = ((tile + 1) ^ 1) - 1
        if 0 <= other < count:
            pairs.append((i, group * count + other))
        elif (group ^ 1) < groups:
            pairs.append((i, (group ^ 1) * count + tile))
    return lax.ppermute(value, ("grp", "tile"), pairs)


def sigmoid_terms(values):
    sigma = jax.nn.sigmoid(values)
    return values * sigma, sigma * (1.0 + values * (1.0 - sigma))


def place():
    tile = lax.axis_index("tile")
    return tile % 2 == 1, tile > 0, tile < lax.axis_size("tile") - 1


def halo_sides(odd, core, cross):
    return jnp.where(odd, cross, core), jnp.where(odd, core, cross)


def exchange_sides(odd, to_next, to_prev):
    return jnp.where(odd, to_prev, to_next), jnp.where(odd, to_next, to_prev)


def row_mask(rows, blk, count):
    block = lax.broadcasted_iota(jnp.int32, (rows, count.shape[1]), 0) // blk
    return (block < count).astype(F32)


def of_kind(values, kind):
    return [values[i : i + 1] for i in range(kind, values.shape[0], KINDS)]


def stacked(rows, blk, fill):
    spare = -len(rows) % 8
    if spare:
        rows = rows + [jnp.full((spare, blk), fill, F32)]
    return jnp.concatenate(rows, axis=0)


def pack_kernel(
    features_in, rows_in, codes_in, near, core_out, cross_out, count_out,
    features, source_rows, codes, done,
):
    copies = []
    for at, (source, target) in enumerate(
        [(rows_in, source_rows), (codes_in, codes), (features_in, features)]
    ):
        copies.append(pltpu.make_async_copy(source, target, done.at[at]))
        copies[-1].start()
    for copy in copies:
        copy.wait()
    offsets, _, blk = source_rows.shape
    per = offsets // KINDS
    count = jnp.where(codes[:1, KINDS - 1 : KINDS] // 2 == 2, 1, 2)
    count = jnp.broadcast_to(count, (1, blk))
    count_out[...] = jnp.broadcast_to(count, count_out.shape)
    both = count == 2
    odd, has_prev, has_next = place()
    diagonal = lax.broadcasted_iota(jnp.int32, (offsets, offsets), 0) == lax.broadcasted_iota(
        jnp.int32, (offsets, offsets), 1
    )
    coded = []
    for j in range(2):
        rows = source_rows[:, j, :]
        block = lax.rem(codes[j : j + 1, :], 2).astype(F32)
        block = jnp.sum(jnp.where(diagonal, block, 0.0), axis=1, keepdims=True)
        live = (rows >= 0) & (count > j)
        coded.append(jnp.where(live, rows.astype(F32) + blk * block, -1.0))
    first, second = coded
    inner = jnp.where(both, first, -1.0)
    rows = of_kind(second, 0) + of_kind(first, 1) + of_kind(second, 1) + of_kind(inner, 2)
    near[...] = stacked(rows, blk, -1.0)
    to_prev = of_kind(jnp.where(has_prev, first, -1.0), 0)
    last = jnp.where(both, second, first)
    to_next = of_kind(jnp.where(has_next, last, -1.0), 2)
    pad = core_out.shape[0] - blk - per
    fill = [jnp.full((pad, blk), -1.0, F32)]
    to_prev = jnp.concatenate(to_prev + fill, axis=0).astype(BF16)
    to_next = jnp.concatenate(to_next + fill, axis=0).astype(BF16)
    front, back = features[:blk, :], features[blk:, :]
    tail = jnp.where(both, back, front)
    core_out[:blk, :], cross_out[:blk, :] = exchange_sides(odd, tail, front)
    core_out[blk:, :], cross_out[blk:, :] = exchange_sides(odd, to_next, to_prev)


def by_targets(columns, at, blk):
    lane = lax.broadcasted_iota(jnp.int32, (blk, blk), 1).astype(F32).astype(BF16)
    one, zero = jnp.ones((blk, blk), BF16), jnp.zeros((blk, blk), BF16)
    entry = jnp.broadcast_to(columns[:, at : at + 1], (blk, blk)).astype(BF16)
    halves = [jnp.where(entry == lane + b * blk, one, zero) for b in range(2)]
    return jnp.concatenate(halves, axis=0)


def by_sources(entries, at, blk):
    sub = lax.broadcasted_iota(jnp.int32, (blk, blk), 0).astype(F32).astype(BF16)
    one, zero = jnp.ones((blk, blk), BF16), jnp.zeros((blk, blk), BF16)
    entry = jnp.broadcast_to(entries[at : at + 1, :], (blk, blk)).astype(BF16)
    halves = [jnp.where(entry == sub + b * blk, one, zero) for b in range(2)]
    return jnp.concatenate(halves, axis=1)


def weights_of(weights, kind, per, axis):
    channels = weights.shape[1]
    parts = []
    for i in range(per):
        at = (i * KINDS + kind) * channels
        parts.append(weights[at : at + channels, :])
    return jnp.concatenate(parts, axis=axis)


def middle_part(pairs, source, weights, picked):
    per, channels = pairs.shape[0], weights.shape[1]
    for i in range(per):
        got = jnp.dot(pairs[i], source, preferred_element_type=F32)
        picked[:, i * channels : (i + 1) * channels] = got.astype(BF16)
    wide = weights_of(weights, 1, per, 0)
    return jnp.dot(picked[...], wide, preferred_element_type=F32)


def outer_part(far, singles, sources, weights, picked):
    per, channels = singles.shape[0] // 2, weights.shape[1]
    for side, source in enumerate(sources):
        for i in range(per):
            at = side * per + i
            select = jnp.concatenate([far[at], singles[at]], axis=1)
            got = jnp.dot(select, source, preferred_element_type=F32)
            picked[:, at * channels : (at + 1) * channels] = got.astype(BF16)
    wide = jnp.concatenate([weights_of(weights, kind, per, 0) for kind in (0, 2)], axis=0)
    return jnp.dot(picked[...], wide, preferred_element_type=F32)


def local_kernel(
    near, features, weights, pairs, singles, pairs_turned, singles_turned, part, picked
):
    blk = near.shape[1]
    per = pairs.shape[0]
    columns = near[...].T
    for i in range(per):
        at, to = per + i, 2 * per + i
        pairs[i, :, :blk] = by_targets(columns, at, blk)
        pairs[i, :, blk:] = by_targets(columns, to, blk)
        pairs_turned[i, :blk, :] = by_sources(near, at, blk)
        pairs_turned[i, blk:, :] = by_sources(near, to, blk)
    part[...] = middle_part(pairs, features[...], weights, picked)
    for i in range(per):
        for side, at in ((0, i), (1, 3 * per + i)):
            singles[side * per + i] = by_targets(columns, at, blk)
            singles_turned[side * per + i] = by_sources(near, at, blk)


def pull_middle(pairs_turned, grads, pulled, base):
    per, channels = pairs_turned.shape[0], grads.shape[1]
    for i in range(per):
        got = jnp.dot(pairs_turned[i], grads, preferred_element_type=F32)
        at = base + i * channels
        pulled[:, at : at + channels] = got.astype(BF16)


def pull_outer(far_turned, singles_turned, grads, pulled, side, base=0):
    per, channels = far_turned.shape[0] // 2, grads.shape[1]
    for i in range(side * per, (side + 1) * per):
        select = jnp.concatenate([far_turned[i], singles_turned[i]], axis=0)
        got = jnp.dot(select, grads, preferred_element_type=F32)
        at = base + i * channels
        pulled[:, at : at + channels] = got.astype(BF16)


def side_of(pulled, side, sides):
    wide = pulled.shape[1] // sides
    return pulled[:, side * wide : (side + 1) * wide]


def source_sums(held, weights, kind):
    per = weights.shape[0] // weights.shape[1] // KINDS
    wide = weights_of(weights, kind, per, 1)
    return lax.dot_general(held, wide, NT, preferred_element_type=F32)


def weight_sums(held, source, wgrad, kind):
    channels = wgrad.shape[1]
    terms = jnp.dot(source.T, held, preferred_element_type=F32)
    for i in range(terms.shape[1] // channels):
        at = (i * KINDS + kind) * channels
        wgrad[at : at + channels, :] = terms[:, i * channels : (i + 1) * channels]


def split_sums(sums, both, blk):
    low, mid, high = sums
    first = mid[:blk] + jnp.where(both, high[blk:], 0.0)
    second = mid[blk:] + low[blk:]
    return jnp.concatenate([first, second], axis=0), low[:blk], high[:blk]


def halves_out(odd, wgrad, keep, send, at):
    shards, slot, _ = keep.shape
    rows = wgrad.shape[0] // shards // 2
    bit = odd.astype(jnp.int32)
    for s in range(shards):
        mine = pl.ds((s * 2 + bit) * rows, rows)
        other = pl.ds((s * 2 + 1 - bit) * rows, rows)
        keep[s, :rows, :] = wgrad[mine, :]
        start = at + s * slot
        send[start : start + rows, :] = wgrad[other, :].astype(BF16)


def first_kernel(
    count_ref, features, core_in, cross_in, singles, part, weights,
    entries, far, halo, hidden, slope, core_out, cross_out, picked,
):
    blk = features.shape[0] // 2
    per = singles.shape[0] // 2
    count = count_ref[:1, :]
    odd, _, _ = place()
    from_next, from_prev = halo_sides(odd, core_in[...].astype(F32), cross_in[...].astype(F32))
    table = stacked([from_next[blk : blk + per], from_prev[blk : blk + per]], blk, -1.0)
    entries[...] = table
    columns = table.T
    for at in range(2 * per):
        far[at] = by_targets(columns, at, blk)
    after, before = from_next[:blk].astype(BF16), from_prev[:blk].astype(BF16)
    halo[0] = after
    halo[1] = before
    front, back = features[:blk, :], features[blk:, :]
    sources = [
        jnp.concatenate([after, back], axis=0),
        jnp.concatenate([before, front], axis=0),
    ]
    pre = part[...] + outer_part(far, singles, sources, weights, picked)
    mask = row_mask(2 * blk, blk, count)
    value, grad = sigmoid_terms(pre)
    field = (value * mask).astype(BF16)
    hidden[...] = field
    slope[...] = grad * mask
    head = field[:blk]
    tail = jnp.where(count == 2, field[blk:], head)
    core_out[...], cross_out[...] = exchange_sides(odd, tail, head)


def middle_kernel(hidden, pairs, entries, weights, part, far_turned, picked):
    part[...] = middle_part(pairs, hidden[...], weights, picked)
    for at in range(far_turned.shape[0]):
        far_turned[at] = by_sources(entries, at, entries.shape[1])


def outer_sources(hidden, odd, core_in, cross_in, blk):
    after, before = halo_sides(odd, core_in[...], cross_in[...])
    low = jnp.concatenate([after, hidden[blk:, :]], axis=0)
    return low, jnp.concatenate([before, hidden[:blk, :]], axis=0)


def second_kernel(
    count_ref, features, hidden, core_in, cross_in, far, singles, part, weights, cotangent,
    far_turned, singles_turned,
    result, grads_out, own_out, pulled, core_out, cross_out, picked,
):
    blk = features.shape[0] // 2
    count = count_ref[:1, :]
    both = count == 2
    odd, _, _ = place()
    low, high = outer_sources(hidden, odd, core_in, cross_in, blk)
    total = part[...] + outer_part(far, singles, [low, high], weights, picked)
    total = total + features[...].astype(F32)
    mask = row_mask(2 * blk, blk, count)
    value, grad = sigmoid_terms(total)
    result[...] = (value * mask).astype(BF16)
    grads = (cotangent[...].astype(F32) * grad * mask).astype(BF16)
    grads_out[...] = grads
    sums = []
    for side, kind in enumerate((0, 2)):
        pull_outer(far_turned, singles_turned, grads, pulled, side)
        sums.append(source_sums(side_of(pulled, side, 2), weights, kind))
    low, high = sums
    own_out[:blk, :] = jnp.where(both, high[blk:], 0.0)
    own_out[blk:, :] = low[blk:]
    core, cross = exchange_sides(odd, low[:blk], high[:blk])
    core_out[...] = core.astype(BF16)
    cross_out[...] = cross.astype(BF16)


def second_rest_kernel(
    hidden, core_in, cross_in, weights, grads, pulled, own_in, pairs_turned,
    own_out, keep, core_out, middle, wgrad,
):
    blk = hidden.shape[0] // 2
    odd, _, _ = place()
    pull_middle(pairs_turned, grads[...], middle, 0)
    own_out[...] = own_in[...] + source_sums(middle[...], weights, 1)
    low, high = outer_sources(hidden, odd, core_in, cross_in, blk)
    weight_sums(middle[...], hidden[...], wgrad, 1)
    weight_sums(side_of(pulled, 0, 2), low, wgrad, 0)
    weight_sums(side_of(pulled, 1, 2), high, wgrad, 2)
    halves_out(odd, wgrad, keep, core_out, 0)


def joined(own, odd, both, core_in, cross_in, blk):
    from_next, from_prev = halo_sides(odd, core_in, cross_in)
    first = own[:blk] + from_prev + jnp.where(both, 0.0, from_next)
    second = own[blk:] + jnp.where(both, from_next, 0.0)
    return jnp.concatenate([first, second], axis=0)


def third_kernel(
    count_ref, features, halo, own, core_in, cross_in, slope,
    far_turned, pairs_turned, singles_turned,
    pulled, keep, core_out, wgrad,
):
    blk = features.shape[0] // 2
    both = count_ref[:1, :] == 2
    odd, _, _ = place()
    core, cross = core_in[...].astype(F32), cross_in[...].astype(F32)
    summed = joined(own[...], odd, both, core, cross, blk)
    grads = (summed * slope[...]).astype(BF16)
    sources = [
        jnp.concatenate([halo[0], features[blk:, :]], axis=0),
        features[...],
        jnp.concatenate([halo[1], features[:blk, :]], axis=0),
    ]
    for side in range(2):
        pull_outer(far_turned, singles_turned, grads, pulled, side)
    pull_middle(pairs_turned, grads, pulled, pulled.shape[1] // KINDS * 2)
    for at, kind in enumerate((0, 2, 1)):
        weight_sums(side_of(pulled, at, KINDS), sources[kind], wgrad, kind)
    halves_out(odd, wgrad, keep, core_out, 0)


def fourth_kernel(count_ref, pulled, weights, grads_in, own_out, core_out, cross_out):
    blk = grads_in.shape[0] // 2
    both = count_ref[:1, :] == 2
    odd, _, _ = place()
    low, high, middle = [
        source_sums(side_of(pulled, at, KINDS), weights, kind)
        for at, kind in enumerate((0, 2, 1))
    ]
    own, to_next, to_prev = split_sums([low, middle, high], both, blk)
    own_out[...] = own + grads_in[...].astype(F32)
    core, cross = exchange_sides(odd, to_next, to_prev)
    core_out[...] = core.astype(BF16)
    cross_out[...] = cross.astype(BF16)


def both_halves(odd, mine, other, scale, out):
    half = out.shape[0] // 2
    mine, other = mine[:half, :].astype(F32) * scale, other[:half, :].astype(F32) * scale
    out[:half, :] = jnp.where(odd, other, mine)
    out[half:, :] = jnp.where(odd, mine, other)


def last_kernel(
    scale, count_ref, own, core_in, cross_in, mine, near, far_off, both_off, input_grad, out
):
    blk = own.shape[0] // 2
    both = count_ref[:1, :] == 2
    odd, _, _ = place()
    core, cross = core_in[...].astype(F32), cross_in[...].astype(F32)
    input_grad[...] = joined(own[...], odd, both, core, cross, blk).astype(BF16)
    upper = (lax.axis_index("tile") // 2) % 2 == 1
    half, part = out.shape[0] // 2, mine.shape[0]
    slot = half + (-half % 16)
    values = [ref[...].astype(F32) * scale for ref in (mine, far_off, near, both_off)]
    low = [jnp.where(upper, values[1], values[0]), jnp.where(upper, values[3], values[2])]
    high = [jnp.where(upper, values[0], values[1]), jnp.where(upper, values[2], values[3])]
    for side in range(2):
        at = side * half
        out[at : at + part, :] = jnp.where(odd, low[1 - side], low[side])
        rest = jnp.where(odd, high[1 - side], high[side])
        skip = 2 * part - slot
        out[at + part : at + half, :] = rest[skip : skip + half - part]


def rows_kernel(scale, mine, other, out):
    odd, _, _ = place()
    both_halves(odd, mine, other, scale, out)


def quarters_kernel(keep, core, kept, send):
    shards, slot, _ = keep.shape
    part = kept.shape[1]
    upper = (lax.axis_index("tile") // 2) % 2 == 1
    for s in range(shards):
        value = keep[s] + core[s * slot : (s + 1) * slot, :].astype(F32)
        low, high = value[:part], value[slot - part :]
        kept[s] = jnp.where(upper, high, low)
        send[s * part : (s + 1) * part, :] = jnp.where(upper, low, high).astype(BF16)


def shards_kernel(keep, core, own, *sends):
    shards, slot, _ = keep.shape
    blk = core.shape[0] - shards * slot
    me = lax.axis_index("grp")
    for d in range(shards):
        to = me ^ d
        at = pl.ds(pl.multiple_of(blk + to * slot, 16), slot)
        value = keep[to] + core[at, :].astype(F32)
        if d == 0:
            own[...] = value
        else:
            sends[d - 1][...] = value.astype(BF16)


def after(first, later):
    return lax.optimization_barrier((first, later))[1]


def added(value, others):
    value = value.astype(F32)
    for other in others:
        value = value + other.astype(F32)
    return value


def call(kernel, outs, *args, scratch=(), micros=1, far=False):
    vmem = pl.BlockSpec(memory_space=pltpu.VMEM)
    return pl.pallas_call(
        kernel,
        out_shape=[jax.ShapeDtypeStruct(shape, kind) for shape, kind in outs],
        in_specs=[pl.BlockSpec(memory_space=pltpu.HBM if far else pltpu.VMEM)] * len(args),
        out_specs=[vmem] * len(outs),
        scratch_shapes=[pltpu.VMEM(*one) if isinstance(one, tuple) else one for one in scratch],
        compiler_params=pltpu.CompilerParams(vmem_limit_bytes=LIMIT),
        cost_estimate=pl.CostEstimate(
            flops=micros * 10**9, bytes_accessed=micros * 3 * 10**6, transcendentals=0
        ),
    )(*args)


def on_device(
    features, source_rows, target_codes, block_count, weight_one, weight_two, out_cotangent
):
    offsets, _, blk = source_rows.shape
    rows, channels = features.shape
    n_grp, n_tile = lax.axis_size("grp"), lax.axis_size("tile")
    per = offsets // KINDS
    flat_one = weight_one.reshape(offsets * channels, channels)
    flat_two = weight_two.reshape(offsets * channels, channels)
    packed = blk + per + (-per % 16)
    half = offsets * channels // n_grp // 2
    slot = half + (-half % 16)
    field, block = ((rows, channels), BF16), ((blk, channels), BF16)
    summed = ((rows, channels), F32)
    keep_shape = ((n_grp, slot, channels), F32)
    core_shape = ((blk + n_grp * slot, channels), BF16)
    pairs_shape = ((per, 2 * blk, 2 * blk), BF16)
    single_shape, turned_shape = ((2 * per, 2 * blk, blk), BF16), ((2 * per, blk, 2 * blk), BF16)
    inner, outer = ((rows, per * channels), BF16), ((rows, 2 * per * channels), BF16)
    pulled = ((rows, offsets * channels), BF16)
    wgrad = ((offsets * channels, channels), F32)

    near, core, cross, count = call(
        pack_kernel,
        [
            ((4 * per + (-4 * per % 8), blk), F32), ((packed, channels), BF16),
            ((packed, channels), BF16), ((8, channels), jnp.int32),
        ],
        *[
            pltpu.with_memory_space_constraint(value, pltpu.HBM)
            for value in (features, source_rows, target_codes.T)
        ],
        scratch=[
            pltpu.VMEM(features.shape, BF16), pltpu.VMEM(source_rows.shape, jnp.int32),
            pltpu.VMEM(target_codes.shape[::-1], jnp.int32),
            pltpu.SemaphoreType.DMA((3,)),
        ],
        micros=3,
        far=True,
    )
    cross, core = crossed(cross), swapped(core, "tile", 1)
    pairs, singles, pairs_turned, singles_turned, part = call(
        local_kernel,
        [pairs_shape, single_shape, pairs_shape, turned_shape, summed],
        near, features, flat_one,
        scratch=[inner],
        micros=2,
    )
    entries, far, halo, hidden, slope, core, cross = call(
        first_kernel,
        [
            ((2 * per + (-2 * per % 8), blk), F32), single_shape, ((2, blk, channels), BF16),
            field, summed, block, block,
        ],
        count, features, core, cross, singles, part, flat_one,
        scratch=[outer],
        micros=2,
    )
    cross, core = crossed(cross), swapped(core, "tile", 1)
    part, far_turned = call(
        middle_kernel,
        [summed, turned_shape],
        hidden, pairs, entries, flat_two,
        scratch=[inner],
        micros=1,
    )
    result, grad_sum, own, held, core_sum, cross_sum = call(
        second_kernel,
        [field, field, summed, outer, block, block],
        count, features, hidden, core, cross, far, singles, part, flat_two, out_cotangent,
        far_turned, singles_turned,
        scratch=[outer],
        micros=3,
    )
    cross_sum, core_sum = crossed(cross_sum), swapped(core_sum, "tile", 1)
    own, keep_two, core_two = call(
        second_rest_kernel,
        [summed, keep_shape, ((n_grp * slot, channels), BF16)],
        hidden, core, cross, flat_two, grad_sum, held, own, pairs_turned,
        scratch=[inner, wgrad],
        micros=1,
    )
    core_two = swapped(core_two, "tile", 1)
    shard = (slot, channels)
    shards = [(shard, F32)] + [(shard, BF16)] * (n_grp - 1)
    part = slot // 2 + (-(slot // 2) % 16)
    quarter = (part, channels)
    steps = [1 << b for b in range(1, (n_tile - 1).bit_length())]
    kept_two, send_two = call(
        quarters_kernel,
        [((n_grp, part, channels), F32), ((n_grp * part, channels), BF16)],
        keep_two, core_two,
    )
    held, keep_one, core_one = call(
        third_kernel,
        [pulled, keep_shape, ((n_grp * slot, channels), BF16)],
        count, features, halo, own, core_sum, cross_sum, slope,
        far_turned, pairs_turned, singles_turned,
        scratch=[wgrad],
        micros=2,
    )
    core_one = swapped(core_one, "tile", 1)
    near_two = swapped(send_two, "tile", steps[0])
    mine_one, *sends_one = call(shards_kernel, shards, keep_one, core_one)
    got_one = [swapped(send, "grp", d + 1) for d, send in enumerate(sends_one)]
    own, core, cross = call(
        fourth_kernel,
        [summed, block, block],
        count, after(sends_one[-1], held), flat_one, grad_sum,
    )
    mine_two, *sends_two = call(
        shards_kernel,
        [(quarter, F32)] + [(quarter, BF16)] * (n_grp - 1),
        after(sends_one[-1], kept_two), near_two,
    )
    got_two = [swapped(send, "grp", d + 1) for d, send in enumerate(sends_two)]
    one = added(mine_one, got_one).astype(BF16)
    two = added(mine_two, got_two)
    for at, bits in enumerate(steps):
        other_one = swapped(one, "tile", bits)
        if at + 1 < len(steps):
            two = two.astype(BF16)
            two = after(one, two)
            other_two = swapped(two, "tile", steps[at + 1])
            two = added(two, [other_two])
            one = added(one, [other_one]).astype(BF16)
    two = two.astype(BF16)
    core, cross = lax.optimization_barrier((one, core, cross))[1:]
    cross, core = crossed(cross), swapped(core, "tile", 1)
    both_off, far_off, near = [swapped(two, "tile", bits) for bits in (steps[0] + 1, steps[0], 1)]
    scale = float(n_grp * n_tile * rows) ** (-0.5)
    shard_out = ((2 * half, channels), F32)
    input_grad, two = call(
        functools.partial(last_kernel, scale),
        [field, shard_out],
        count, own, core, cross, two, near, far_off, both_off,
    )
    one = added(one, [other_one]).astype(BF16)
    (one,) = call(
        functools.partial(rows_kernel, scale), [shard_out], one, swapped(one, "tile", 1)
    )
    return (result, input_grad, one, two)


def solution(mesh):
    in_specs = (
        P(("grp", "tile"), None),
        P(None, ("grp", "tile"), None),
        P(None, ("grp", "tile")),
        P(("grp", "tile")),
        P(),
        P(),
        P(("grp", "tile"), None),
    )
    out_specs = (P(("grp", "tile"), None), P(("grp", "tile"), None), P("grp", None), P("grp", None))
    return jax.shard_map(
        on_device, mesh=mesh, in_specs=in_specs, out_specs=out_specs, check_vma=False
    )
```
